512 devices in a mesh: dp: 8 (over z_lo), seq: 64 (over y, z_hi, x, core).
Axes of the slice: x: 4, y: 4, z: 16 (z_hi: 2, z_lo: 8; z = z_hi * 8 + z_lo), core: 2. Of those that a mesh axis runs over, the one named last changes fastest.
Arguments:
- activations: bfloat16 [8, 64, 512, 1024], P('dp', 'seq'), may hold values from -6 to 6
- cotangent: bfloat16 [8, 64, 512, 1024], P('dp', 'seq'), may hold values from -6 to 6
- inner_weight: bfloat16 [64, 512, 512], P('seq'), may hold values from -0.25 to 0.25
- outer_weight: bfloat16 [512, 64, 64], P('seq'), may hold values from -0.75 to 0.75
Outputs:
- input_grad: bfloat16 [8, 64, 512, 1024], P('dp', 'seq')
- inner_grad: float32 [64, 512, 512], P('seq')
- outer_grad: float32 [512, 64, 64], P('seq')
The draws below stay inside these ranges and needn't reach their ends.
All inputs are finite; a program needn't handle non-finite values.
Results may differ from the reference program's by a relative error of at most 0.0049.
Values may be sent and summed in bfloat16 or wider, within the bound.
A program may use at most 64 MiB of HBM per device.

```python
import jax
import jax.numpy as jnp
from jax import lax

D = 1024
BS = 512
NB = 64
SEQS = 8


def levels(own_key, extent, cuts, least, top_value):
    loudness, own = 1.0, jax.random.fold_in(own_key, 6)
    for position, shards_of in cuts:
        draws = jnp.exp(jax.random.uniform(jax.random.fold_in(own, position), (shards_of,), jnp.float32, least / len(cuts), top_value / len(cuts)))
        loudness = loudness * jnp.repeat(draws, extent[position] // shards_of).reshape([-1 if axis == position else 1 for axis in range(len(extent))])
    return loudness


def gaussian(rng, shape, spread, bound, cuts=(), kind=jnp.bfloat16):
    result = spread * jax.random.normal(rng, shape, jnp.float32)
    if cuts:
        result = result * levels(rng, shape, cuts, -0.22, 0.18)
    return jnp.clip(result, -bound, bound).astype(kind)


def setup_inputs(seed: int = 0) -> dict:
    seeds = jax.random.split(jax.random.key(seed), 5)
    activations = gaussian(seeds[0], (SEQS, NB, BS, D), 1.0, 6.0, ((0, 8), (1, 64)))
    cotangent = gaussian(seeds[1], (SEQS, NB, BS, D), 1.0, 6.0, ((0, 8), (1, 64)))
    inner_weight = gaussian(seeds[2], (NB, BS, BS), BS ** -0.5, 0.25, ((0, 64),))
    outer_weight = gaussian(seeds[3], (BS, NB, NB), NB ** -0.5, 0.75, ((0, 64),))
    return dict(activations=activations, cotangent=cotangent, inner_weight=inner_weight, outer_weight=outer_weight)


def reference(activations, cotangent, inner_weight, outer_weight):
    rows = lax.broadcasted_iota(jnp.int32, (BS, BS), 0)
    cols = lax.broadcasted_iota(jnp.int32, (BS, BS), 1)
    tril = (rows >= cols).astype(jnp.float32)
    brows = lax.broadcasted_iota(jnp.int32, (NB, NB), 0)
    bcols = lax.broadcasted_iota(jnp.int32, (NB, NB), 1)
    low = (brows >= bcols).astype(jnp.float32)
    inner = (inner_weight * tril.astype(jnp.bfloat16)[None]).astype(jnp.float32)
    outer = (outer_weight * low.astype(jnp.bfloat16)[None]).astype(jnp.float32)

    def one_sequence(carry, pieces):
        inputs, grads = pieces
        inputs32 = inputs.astype(jnp.float32)
        grads32 = grads.astype(jnp.float32)
        mixed = jnp.einsum('nij,njc->nic', inner, inputs32).astype(jnp.bfloat16).astype(jnp.float32)
        mixed_grad = jnp.einsum('pbe,bpc->epc', outer, grads32).astype(jnp.bfloat16).astype(jnp.float32)
        input_grad = jnp.einsum('nij,nic->njc', inner, mixed_grad).astype(jnp.bfloat16)
        inner_part = jnp.einsum('nic,njc->nij', mixed_grad, inputs32)
        outer_part = jnp.einsum('bpc,epc->pbe', grads32, mixed)
        return ((carry[0] + inner_part, carry[1] + outer_part), input_grad)
    start = (jnp.zeros((NB, BS, BS), jnp.float32), jnp.zeros((BS, NB, NB), jnp.float32))
    totals, input_grad = lax.scan(one_sequence, start, (activations, cotangent))
    scale = jnp.sqrt(jnp.float32(SEQS * D))
    inner_grad = totals[0] * tril[None] / scale
    outer_grad = totals[1] * low[None] / scale
    return (input_grad, inner_grad, outer_grad)
```

```python
import functools
import math

import jax
import jax.numpy as jnp
from jax import lax
from jax.experimental import pallas as pl
from jax.experimental.pallas import tpu as pltpu
from jax.sharding import PartitionSpec as P

MESH = pl.DeviceIdType.MESH
BF = jnp.bfloat16
F32 = jnp.float32

B = 512
D = 1024
NC = 4
CW = D // NC
PD = 32
PP = 16
NZ = 16
OFFS = (0, 128, 384, 768)
PACK = 1280


def coords():
    lo = lax.axis_index("dp")
    s = lax.axis_index("seq")
    core = lax.rem(s, 2)
    x = lax.rem(s // 2, 4)
    h = lax.rem(s // 8, 2)
    y = s // 16
    return lo, y, h, x, core


def plane_peer(i):
    lo, y, h, x, core = coords()
    px = lax.rem(x + lax.rem(i // 2, 4), 4)
    py = lax.rem(y + i // 8, 4)
    pc = lax.rem(core + i, 2)
    return py * 8 + px * 2 + pc, (lo, py * 16 + h * 8 + px * 2 + pc)


def ring_peer(i):
    lo, y, h, x, core = coords()
    z = lax.rem(h * 8 + lo + i, NZ)
    return z, (lax.rem(z, 8), y * 16 + (z // 8) * 8 + x * 2 + core)


def dp_peer(i):
    lo, y, h, x, core = coords()
    t = lax.rem(lo + i, 8)
    return t, (t, y * 16 + h * 8 + x * 2 + core)


def remote(src, dst, send, recv, device):
    return pltpu.make_async_remote_copy(
        src_ref=src, dst_ref=dst, send_sem=send, recv_sem=recv, device_id=device, device_id_type=MESH
    )


def wait_bytes(ref, sem):
    pltpu.make_async_copy(ref, ref, sem).wait()


def iota(shape, dim):
    return lax.broadcasted_iota(jnp.int32, shape, dim)


def dot_nt(a, b):
    return lax.dot_general(a, b, (((1,), (1,)), ((), ())), preferred_element_type=F32)


def dot_nn(a, b):
    return lax.dot_general(a, b, (((1,), (0,)), ((), ())), preferred_element_type=F32)


def dot_tn(a, b):
    return lax.dot_general(a, b, (((0,), (0,)), ((), ())), preferred_element_type=F32)


def halves(a, b):
    first = jnp.concatenate([a[:8], b[:8]], axis=0)
    second = jnp.concatenate([a[8:], b[8:]], axis=0)
    return first.astype(BF), second.astype(BF)


def kernel(
    act, cot, inner, outer, ig_out, inner_out, outer_out,
    cot_s, blk, x_s, x_r, g_s, g_r, inner_p, inner_t, ow, tmat, wmat, s_acc, i_acc,
    rs_s, rs_r, ag, ss_s, ss_r, sg,
    c_ss, c_rs, z_ss, z_rs, x_ss, x_rs, g_ss, g_rs, o_sem, rs_sem, ag_sem, ss_sem, sg_sem,
):
    lo, y, h, x, core = coords()
    me = y * 8 + x * 2 + core
    zme = h * 8 + lo
    scale = 1.0 / math.sqrt(8192.0)

    barrier = pltpu.get_barrier_semaphore()

    @pl.loop(1, PD)
    def _(i):
        pl.semaphore_signal(barrier, inc=1, device_id=plane_peer(i)[1], device_id_type=MESH)

    @pl.loop(1, NZ)
    def _(i):
        pl.semaphore_signal(barrier, inc=1, device_id=ring_peer(i)[1], device_id_type=MESH)

    @pl.loop(0, 16)
    def _(q):
        big, u = q // 4, lax.rem(q, 4)
        at = pl.multiple_of(big * 128 + u * 16, 16)
        a = cot[pl.ds(at, 16), :].astype(F32)
        b = cot[pl.ds(at + 64, 16), :].astype(F32)
        first, second = halves(a, b)
        for k in range(NC):
            cot_s[k, big * 8 + u * 2] = first[:, k * CW:(k + 1) * CW]
            cot_s[k, big * 8 + u * 2 + 1] = second[:, k * CW:(k + 1) * CW]

    pl.semaphore_wait(barrier, PD - 1 + NZ - 1)

    def a2a_start(src, dst, send, recv):
        @pl.loop(1, PD)
        def _(i):
            d, device = plane_peer(i)
            remote(src(d), dst(me), send, recv, device).start()

        pltpu.make_async_copy(src(me), dst(me), recv).start()

    mine = h * PD
    for k in range(NC):
        a2a_start(lambda d: cot_s.at[k, d], lambda d: blk.at[k, mine + d], c_ss.at[k], c_rs.at[k])
        if k == 0:
            pltpu.make_async_copy(outer, ow.at[h], o_sem.at[2]).start()
            remote(outer, ow.at[h], o_sem.at[0], o_sem.at[1], ring_peer(8)[1]).start()

    def cross(k, part):
        rows = pl.ds(mine + part * 8, 8)
        return remote(blk.at[k, rows], blk.at[k, rows], z_ss.at[k, part], z_rs.at[k, part], ring_peer(8)[1])

    for k in range(NC):
        wait_bytes(blk.at[k, pl.ds(mine, PD)], c_rs.at[k])
        for part in range(4):
            cross(k, part).start()

    @pl.loop(0, 16)
    def _(q):
        big, u = q // 4, lax.rem(q, 4)
        at = pl.multiple_of(big * 128 + u * 16, 16)

        def rows(start):
            v = inner[pl.ds(start, 16), :].astype(F32)
            return jnp.where(iota((16, B), 0) + start >= iota((16, B), 1), v, 0.0)

        first, second = halves(rows(at), rows(at + 64))
        to = pl.multiple_of(big * 128 + u * 32, 32)
        inner_p[pl.ds(to, 16), :] = first
        inner_p[pl.ds(to + 16, 16), :] = second

    inner_t[...] = inner_p[...].T

    @pl.loop(0, 4)
    def _(q):
        rows = pl.ds(pl.multiple_of(q * 128, 128), 128)
        v = dot_nn(inner_p[rows, :], act[...]).astype(BF)
        x_s[pl.ds(q * 8, 8)] = v.reshape(8, PP, D)

    a2a_start(lambda d: x_s.at[d], lambda d: x_r.at[d], x_ss, x_rs)

    pltpu.make_async_copy(outer, ow.at[h], o_sem.at[2]).wait()
    wait_bytes(ow.at[1 - h], o_sem.at[1])
    pick = (iota((32, 64), 1) == 16 * (iota((32, 64), 0) // 8) + 8 * h + lax.rem(iota((32, 64), 0), 8)).astype(BF)
    low = (iota((64, 64), 0) >= iota((64, 64), 1)).astype(F32)
    for hh in range(2):
        @pl.loop(0, 8)
        def _(t):
            v = (ow[hh, t].astype(F32) * low).astype(BF)
            tmat[hh * 8 + t] = dot_nt(pick, v).astype(BF)

    n_r = iota((128, 512), 0)
    n_c = iota((128, 512), 1)
    e_r = iota((64, 1024), 0)
    e_c = iota((64, 1024), 1) // 16
    bl = lax.rem(e_c, 32)
    spread = (e_r == 16 * (bl // 8) + 8 * (e_c // 32) + lax.rem(bl, 8)).astype(BF)

    @pl.loop(0, 4)
    def _(q):
        row = n_r + q * 128
        perm = (n_c == lax.rem(row, 16) * 32 + row // 16).astype(BF)
        t2 = dot_nn(perm, tmat[...].reshape(512, 64)).astype(BF)
        w = dot_nn(t2, spread)
        same = lax.rem(iota((128, 1024), 0), 16) == lax.rem(iota((128, 1024), 1), 16)
        wmat[pl.ds(pl.multiple_of(q * 128, 128), 128), :] = jnp.where(same, w, 0.0).astype(BF)

    def mix(k):
        wait_other = pl.ds((1 - h) * PD, PD)
        for part in range(4):
            rows = pl.ds((1 - h) * PD + part * 8, 8)
            wait_bytes(blk.at[k, rows], z_rs.at[k, part])

        @pl.loop(0, 4)
        def _(q):
            rows = pl.ds(pl.multiple_of(q * 128, 128), 128)
            v = dot_nn(wmat[rows, :], blk[k].reshape(1024, CW)).astype(BF)
            g_s[k, pl.ds(q * 8, 8)] = v.reshape(8, PP, CW)

        a2a_start(lambda d: g_s.at[k, d], lambda d: g_r.at[k, d], g_ss.at[k], g_rs.at[k])

    def outer_part(k):
        if k == 0:
            wait_bytes(x_r, x_rs)

        @pl.loop(0, 8)
        def _(q):
            rows = pl.ds(pl.multiple_of(q * 128, 128), 128)
            v = dot_nt(blk[k, pl.ds(q * 8, 8)].reshape(128, CW), x_r[:, :, k * CW:(k + 1) * CW].reshape(512, CW))
            if k == 0:
                s_acc[rows, :] = v
            else:
                s_acc[rows, :] += v

    def back(k):
        wait_bytes(g_r.at[k], g_rs.at[k])
        cols = slice(k * CW, (k + 1) * CW)

        @pl.loop(0, 4)
        def _(q):
            rows = pl.ds(pl.multiple_of(q * 128, 128), 128)
            v = dot_nt(g_r[k, pl.ds(q * 8, 8)].reshape(128, CW), act[:, cols])
            if k == 0:
                i_acc[rows, :] = v
            else:
                i_acc[rows, :] += v

    def back_input(k):
        cols = slice(k * CW, (k + 1) * CW)

        @pl.loop(0, 4)
        def _(q):
            rows = pl.ds(pl.multiple_of(q * 128, 128), 128)
            ig_out[rows, cols] = dot_nn(inner_t[rows, :], g_r[k].reshape(512, CW)).astype(BF)

    inner_out[...] = jnp.zeros_like(inner_out)

    for k in range(NC):
        mix(k)
        outer_part(k)
        if k > 0:
            back(k - 1)
            back_input(k - 1)

    packed = jnp.zeros((256, 128), F32)
    same = lax.rem(iota((256, 512), 0), 16) == lax.rem(iota((256, 512), 1), 16)
    for bh in range(4):
        v = jnp.where(same, s_acc[bh * 256:(bh + 1) * 256, :], 0.0).astype(BF)
        put = (iota((512, 128), 1) == 32 * bh + iota((512, 128), 0) // 16).astype(BF)
        packed = packed + dot_nn(v, put)
    ss_s[...] = packed.astype(BF).reshape(8, 32, 128)

    def scatter(src, dst, sem):
        @pl.loop(1, 8)
        def _(i):
            t, device = dp_peer(i)
            remote(src.at[t], dst.at[lo], sem.at[0], sem.at[1], device).start()

        pltpu.make_async_copy(src.at[lo], dst.at[lo], sem.at[1]).start()

    scatter(ss_s, ss_r, ss_sem)

    back(NC - 1)
    for big in range(4):
        w = 128 * (big + 1)
        v = i_acc[big * 128:(big + 1) * 128, :w].astype(BF)
        rs_s[:, :, OFFS[big]:OFFS[big] + w] = v.reshape(8, 16, w)
    scatter(rs_s, rs_r, rs_sem)
    back_input(NC - 1)

    wait_bytes(ss_r, ss_sem.at[1])
    total = ss_r[0].astype(F32)
    for i in range(1, 8):
        total = total + ss_r[i].astype(F32)
    sg[zme] = total.astype(BF)

    @pl.loop(1, NZ)
    def _(i):
        remote(sg.at[zme], sg.at[zme], sg_sem.at[0], sg_sem.at[1], ring_peer(i)[1]).start()

    wait_bytes(rs_r, rs_sem.at[1])
    total = rs_r[0].astype(F32)
    for i in range(1, 8):
        total = total + rs_r[i].astype(F32)
    ag[lo] = total.astype(BF)

    @pl.loop(1, 8)
    def _(i):
        remote(ag.at[lo], ag.at[lo], ag_sem.at[0], ag_sem.at[1], dp_peer(i)[1]).start()

    wait_bytes(sg.at[pl.ds(0, NZ - 1)], sg_sem.at[1])
    parts = []
    for hs in range(2):
        v = sg[hs * 8:(hs + 1) * 8].astype(F32).reshape(16, 16, 128)
        v = jnp.where(h == 0, v[:, :8], v[:, 8:])
        parts.append(v.reshape(128, 128).astype(BF))
    c_r = iota((128, 64), 0)
    c_c = iota((128, 64), 1)
    for bh in range(4):
        v = jnp.zeros((128, 64), F32)
        for hs in range(2):
            el = c_r - 32 * bh
            col = (el >= 0) & (el < 32) & (c_c == 16 * (el // 8) + 8 * hs + lax.rem(el, 8))
            v = v + dot_nn(parts[hs], col.astype(BF))
        for g in range(2):
            base = 32 * (bh % 2) + 16 * g + 8 * (bh // 2)
            keep = iota((8, 8, 64), 0) + base >= iota((8, 8, 64), 2)
            outer_out[base:base + 8] = jnp.where(keep, v[64 * g:64 * g + 64].reshape(8, 8, 64) * scale, 0.0)

    wait_bytes(ag.at[pl.ds(0, 7)], ag_sem.at[1])
    for big in range(4):
        w = 128 * (big + 1)
        v = ag[:, :, OFFS[big]:OFFS[big] + w].astype(F32)
        for hh in range(2):
            start = big * 128 + hh * 64
            part = v[:, 8 * hh:8 * hh + 8, :].reshape(64, w) * scale
            keep = iota((64, w), 0) + start >= iota((64, w), 1)
            inner_out[start:start + 64, :w] = jnp.where(keep, part, 0.0)

    for k in range(NC):
        wait_bytes(cot_s.at[k, pl.ds(0, PD - 1)], c_ss.at[k])
        wait_bytes(g_s.at[k, pl.ds(0, PD - 1)], g_ss.at[k])
        for part in range(4):
            cross(k, part).wait_send()
    wait_bytes(x_s.at[pl.ds(0, PD - 1)], x_ss)
    wait_bytes(outer, o_sem.at[0])
    wait_bytes(ss_s.at[pl.ds(0, 7)], ss_sem.at[0])
    wait_bytes(rs_s.at[pl.ds(0, 7)], rs_sem.at[0])
    wait_bytes(ag.at[pl.ds(0, 7)], ag_sem.at[0])
    wait_bytes(sg.at[pl.ds(0, NZ - 1)], sg_sem.at[0])


def local(activations, cotangent, inner_weight, outer_weight):
    vmem = pl.BlockSpec(memory_space=pltpu.VMEM)
    dma = pltpu.SemaphoreType.DMA
    scratch = [
        pltpu.VMEM((NC, PD, PP, CW), BF),
        pltpu.VMEM((NC, 2 * PD, PP, CW), BF),
        pltpu.VMEM((PD, PP, D), BF),
        pltpu.VMEM((PD, PP, D), BF),
        pltpu.VMEM((NC, PD, PP, CW), BF),
        pltpu.VMEM((NC, PD, PP, CW), BF),
        pltpu.VMEM((B, B), BF),
        pltpu.VMEM((B, B), BF),
        pltpu.VMEM((2, 8, 64, 64), BF),
        pltpu.VMEM((16, 32, 64), BF),
        pltpu.VMEM((512, 1024), BF),
        pltpu.VMEM((1024, 512), F32),
        pltpu.VMEM((B, B), F32),
        pltpu.VMEM((8, 16, PACK), BF),
        pltpu.VMEM((8, 16, PACK), BF),
        pltpu.VMEM((8, 16, PACK), BF),
        pltpu.VMEM((8, 32, 128), BF),
        pltpu.VMEM((8, 32, 128), BF),
        pltpu.VMEM((NZ, 32, 128), BF),
        dma((NC,)), dma((NC,)),
        dma((NC, 4)), dma((NC, 4)),
        dma, dma,
        dma((NC,)), dma((NC,)),
        dma((3,)), dma((2,)), dma((2,)), dma((2,)), dma((2,)),
    ]
    ig, inner_grad, outer_grad = pl.pallas_call(
        kernel,
        out_shape=(
            jax.ShapeDtypeStruct((B, D), BF),
            jax.ShapeDtypeStruct((B, B), F32),
            jax.ShapeDtypeStruct((64, 8, 64), F32),
        ),
        in_specs=[vmem] * 4,
        out_specs=(vmem, vmem, vmem),
        scratch_shapes=scratch,
        compiler_params=pltpu.CompilerParams(
            collective_id=0, has_side_effects=True, vmem_limit_bytes=48 * 1024 * 1024
        ),
        cost_estimate=pl.CostEstimate(flops=8_000_000_000, bytes_accessed=6_000_000, transcendentals=0),
        name="mixer",
    )(activations[0, 0], cotangent[0, 0], inner_weight[0], outer_weight)
    return ig[None, None], inner_grad[None], jnp.transpose(outer_grad, (1, 0, 2))


def solution(mesh):
    placed = (
        P("dp", "seq", None, None),
        P("dp", "seq", None, None),
        P("seq", None, None),
        P("seq", None, None),
    )
    return jax.shard_map(
        local,
        mesh=mesh,
        in_specs=placed,
        out_specs=(P("dp", "seq", None, None), P("seq", None, None), P("seq", None, None)),
        check_vma=False,
    )
```

```python
import functools
import math

import jax
import jax.numpy as jnp
from jax import lax
from jax.experimental import pallas as pl
from jax.experimental.pallas import tpu as pltpu
from jax.sharding import PartitionSpec as P

MESH = pl.DeviceIdType.MESH
BF = jnp.bfloat16
F32 = jnp.float32

B = 512
D = 1024
NI = 4
CW = D // NI
PD = 32
PP = 16
NZ = 16
OFFS = (0, 128, 384, 768)
ORDER = (3, 2, 1, 0)
PARTS = 4
PACK = 1280


def coords():
    lo = lax.axis_index("dp")
    s = lax.axis_index("seq")
    core = lax.rem(s, 2)
    x = lax.rem(s // 2, 4)
    h = lax.rem(s // 8, 2)
    y = s // 16
    return lo, y, h, x, core


def plane_peers():
    lo, y, h, x, core = coords()
    offs = []
    for b in range(4):
        for c in range(2):
            offs.append(lax.rem(x + b, 4) * 2 + lax.rem(core + c, 2))

    def row(a):
        py = lax.rem(y + a, 4)
        return py * 8, py * 16 + h * 8

    return row, offs, lo


def ring_peer(i):
    lo, y, h, x, core = coords()
    z = lax.rem(h * 8 + lo + i, NZ)
    return z, (lax.rem(z, 8), y * 16 + (z // 8) * 8 + x * 2 + core)


def dp_peer(i):
    lo, y, h, x, core = coords()
    t = lax.rem(lo + i, 8)
    return t, (t, y * 16 + h * 8 + x * 2 + core)


def remote(src, dst, send, recv, device):
    return pltpu.make_async_remote_copy(
        src_ref=src, dst_ref=dst, send_sem=send, recv_sem=recv, device_id=device, device_id_type=MESH
    )


def wait_bytes(ref, sem):
    pltpu.make_async_copy(ref, ref, sem).wait()


def iota(shape, dim):
    return lax.broadcasted_iota(jnp.int32, shape, dim)


def dot_nt(a, b):
    return lax.dot_general(a, b, (((1,), (1,)), ((), ())), preferred_element_type=F32)


def dot_nn(a, b):
    return lax.dot_general(a, b, (((1,), (0,)), ((), ())), preferred_element_type=F32)


def dot_tn(a, b):
    return lax.dot_general(a, b, (((0,), (0,)), ((), ())), preferred_element_type=F32)


def halves(a, b):
    first = jnp.concatenate([a[:8], b[:8]], axis=0)
    second = jnp.concatenate([a[8:], b[8:]], axis=0)
    return first.astype(BF), second.astype(BF)


def kernel(
    act_in, cot_in, inner_in, outer_in, ig_res, ag_res, sg_res,
    act, cot, inner, outer, cot_s, blk, g_s, g_r, x_s, x_r, inner_p, inner_t,
    oscr, ot, ow, wmat, ig_out, ig_acc, rs_s, rs_r, ag, sy_s, sy_r, ss_s, ss_r, sg,
    in_sem, c_ss, c_rs, z_ss, z_rs, x_sem, g_ss, g_rs, o_ss, o_rs, rs_ss, rs_rs, ag_ss, ag_rs,
    sy_ss, sy_rs, ss_sem, sg_sem, out_sem,
):
    lo, y, h, x, core = coords()
    me = y * 8 + x * 2 + core
    zme = h * 8 + lo
    peer_row, peer_offs, _ = plane_peers()
    mine = h * PD
    other = (1 - h) * PD

    def column_peer(a):
        py = lax.rem(y + a, 4)
        return py, (lo, py * 16 + h * 8 + x * 2 + core)

    loads = [
        pltpu.make_async_copy(a, b, in_sem.at[n])
        for n, (a, b) in enumerate(((cot_in, cot), (outer_in, outer), (inner_in, inner), (act_in, act)))
    ]
    for load in loads:
        load.start()

    barrier = pltpu.get_barrier_semaphore()

    @pl.loop(1, NZ)
    def _(i):
        pl.semaphore_signal(barrier, inc=1, device_id=ring_peer(i)[1], device_id_type=MESH)

    def plane_loop(body):
        @pl.loop(0, 4)
        def _(a):
            place, seq = peer_row(a)
            for off in peer_offs[1:]:
                body(place + off, (lo, seq + off))

        @pl.loop(1, 4)
        def _(a):
            place, seq = peer_row(a)
            body(place + peer_offs[0], (lo, seq + peer_offs[0]))

    plane_loop(lambda d, device: pl.semaphore_signal(barrier, inc=1, device_id=device, device_id_type=MESH))

    loads[0].wait()

    @pl.loop(0, 16)
    def _(q):
        big, u = q // 4, lax.rem(q, 4)
        at = pl.multiple_of(big * 128 + u * 16, 16)
        a = cot[pl.ds(at, 16), :].astype(F32)
        b = cot[pl.ds(at + 64, 16), :].astype(F32)
        first, second = halves(a, b)
        for quarter in range(4):
            cols = slice(quarter * CW, (quarter + 1) * CW)
            cot_s[big, quarter * 8 + u * 2] = first[:, cols]
            cot_s[big, quarter * 8 + u * 2 + 1] = second[:, cols]

    loads[1].wait()
    low = iota((64, 64), 0) >= iota((64, 64), 1)
    for t in range(8):
        v = jnp.where(low, outer[t].astype(F32), 0.0)
        oscr[pl.ds(t, 32, stride=8), :] = jnp.concatenate([v[:32], v[32:]], axis=1)
    ot[...] = oscr[...].astype(BF)

    pl.semaphore_wait(barrier, PD - 1 + NZ - 1)

    def a2a_start(src, dst, send, recv):
        plane_loop(lambda d, device: remote(src(d), dst(me), send, recv, device).start())
        pltpu.make_async_copy(src(me), dst(me), recv).start()

    def cross(t, part):
        size = PD // PARTS
        rows = blk.at[ORDER[t], pl.ds(mine + part * size, size)]
        return remote(rows, rows, z_ss.at[t, part], z_rs.at[t, part], ring_peer(8)[1])

    def cross_start(t):
        @pl.when(h == 1)
        def _():
            cross(t, 0).start()

        for part in range(1, PARTS):
            cross(t, part).start()

    def cross_wait(t):
        size = PD // PARTS
        @pl.when(h == 0)
        def _():
            wait_bytes(blk.at[ORDER[t], pl.ds(other, size)], z_rs.at[t, 0])

        for part in range(1, PARTS):
            wait_bytes(blk.at[ORDER[t], pl.ds(other + part * size, size)], z_rs.at[t, part])

    def own_start(t):
        k = ORDER[t]
        a2a_start(lambda d: cot_s.at[k, d], lambda d: blk.at[k, mine + d], c_ss.at[t], c_rs.at[t])

    def own_wait(t):
        wait_bytes(blk.at[ORDER[t], pl.ds(mine, PD)], c_rs.at[t])

    for t in range(NI):
        own_start(t)
        if t == 0:
            for a in range(1, 4):
                remote(ot, ow.at[y, h], o_ss.at[a], o_rs.at[a], column_peer(a)[1]).start()
            remote(ot, ow.at[y, h], o_ss.at[0], o_rs.at[0], ring_peer(8)[1]).start()
            own_copy = pltpu.make_async_copy(ot, ow.at[y, h], o_rs.at[7])
            own_copy.start()
        if t > 0:
            own_wait(t - 1)
            cross_start(t - 1)
    own_wait(NI - 1)
    cross_start(NI - 1)

    loads[2].wait()

    @pl.loop(0, 16)
    def _(q):
        big, u = q // 4, lax.rem(q, 4)
        at = pl.multiple_of(big * 128 + u * 16, 16)

        def rows(start):
            v = inner[pl.ds(start, 16), :].astype(F32)
            return jnp.where(iota((16, B), 0) + start >= iota((16, B), 1), v, 0.0)

        first, second = halves(rows(at), rows(at + 64))
        to = pl.multiple_of(big * 128 + u * 32, 32)
        inner_p[pl.ds(to, 16), :] = first
        inner_p[pl.ds(to + 16, 16), :] = second

    inner_t[...] = inner_p[...].T
    loads[3].wait()

    @pl.loop(0, 4)
    def _(q):
        rows = pl.ds(pl.multiple_of(q * 128, 128), 128)
        v = dot_nn(inner_p[rows, :], act[...]).astype(BF)
        for quarter in range(4):
            cols = slice(quarter * CW, (quarter + 1) * CW)
            x_s[quarter * 8:(quarter + 1) * 8, q] = v[:, cols].reshape(8, PP, CW)

    a2a_start(lambda d: x_s.at[d], lambda d: x_r.at[d], x_sem.at[0], x_sem.at[1])

    def outer_pass():
        wait_bytes(ow.at[y, 1 - h], o_rs.at[0])
        for a in range(1, 4):
            remote(ow.at[y, 1 - h], ow.at[y, 1 - h], o_ss.at[3 + a], o_rs.at[3 + a], column_peer(a)[1]).start()

    def outer_wait():
        own_copy.wait()
        for a in range(1, 4):
            src = lax.rem(y + 4 - a, 4)
            wait_bytes(ow.at[src, h], o_rs.at[a])
            wait_bytes(ow.at[src, 1 - h], o_rs.at[3 + a])

    def build(k):
        el = iota((64, 512), 1) // 16
        pick = (iota((64, 512), 0) == 16 * (el // 8) + 8 * h + lax.rem(el, 8)).astype(BF)
        same = lax.rem(iota((128, 512), 0), 16) == lax.rem(iota((128, 512), 1), 16)

        @pl.loop(0, 8)
        def _(g):
            group = 2 * lax.rem(g, 4) + g // 4
            rows = pl.ds(pl.multiple_of(lax.rem(group, 4) * 64, 64), 64)
            both = []
            for hh in range(2):
                v = ow[k, hh, rows, :].astype(F32)
                both.append(jnp.where(group < 4, v[:, :64], v[:, 64:]).reshape(8, 8, 64))
            v = jnp.concatenate(both, axis=1).reshape(128, 64).astype(BF)
            w = jnp.where(same, dot_nn(v, pick), 0.0).astype(BF)
            wmat[k, :, pl.ds(pl.multiple_of(g * 128, 128), 128)] = w.T

    def mix(t):
        k = ORDER[t]
        cross_wait(t)

        @pl.loop(0, 4)
        def _(a):
            place, seq = peer_row(a)
            rows = pl.ds(pl.multiple_of(place * PP, 128), 128)
            v = dot_nn(wmat[k, rows, :], blk[k].reshape(1024, CW)).astype(BF)
            g_s[k, pl.ds(place, 8)] = v.reshape(8, PP, CW)

            def give(off):
                remote(
                    g_s.at[k, place + off], g_r.at[k, me], g_ss.at[t], g_rs.at[t], (lo, seq + off)
                ).start()

            for off in peer_offs[1:]:
                give(off)

            @pl.when(a > 0)
            def _():
                give(peer_offs[0])

        pltpu.make_async_copy(g_s.at[k, me], g_r.at[k, me], g_rs.at[t]).start()

    def outer_part(t):
        k = ORDER[t]
        if t == 0:
            wait_bytes(x_r, x_sem.at[1])
        same = lax.rem(iota((128, 512), 0), 16) == lax.rem(iota((128, 512), 1), 16)

        @pl.loop(0, 2)
        def _(half):
            total = jnp.zeros((128, 128), F32)
            for bh in range(4):
                v = dot_nt(blk[k, pl.ds(bh * 16 + half * 8, 8)].reshape(128, CW), x_r[:, k].reshape(512, CW))
                put = (iota((512, 128), 1) == 32 * bh + iota((512, 128), 0) // 16).astype(BF)
                total = total + dot_nn(jnp.where(same, v, 0.0).astype(BF), put)
            sy_s[k, pl.ds(pl.multiple_of(half * 128, 128), 128), :] = total.astype(BF)

        @pl.when(y == k)
        def _():
            pltpu.make_async_copy(sy_s.at[k], sy_r.at[y], sy_rs.at[y]).start()

        @pl.when(y != k)
        def _():
            device = (lo, k * 16 + h * 8 + x * 2 + core)
            remote(sy_s.at[k], sy_r.at[y], sy_ss.at[k], sy_rs.at[y], device).start()

    def back(t):
        k = ORDER[t]
        w = 128 * (k + 1)
        wait_bytes(g_r.at[k], g_rs.at[t])
        v = jnp.zeros((128, w), F32)
        for quarter in range(4):
            cols = slice(quarter * CW, (quarter + 1) * CW)
            v = v + dot_nt(g_r[k, quarter * 8:(quarter + 1) * 8].reshape(128, CW), act[:w, cols])
        cols = slice(OFFS[k], OFFS[k] + w)
        rs_s[:, :, cols] = v.astype(BF).reshape(8, 16, w)

        @pl.loop(1, 8)
        def _(i):
            to, device = dp_peer(i)
            remote(rs_s.at[to, :, cols], rs_r.at[lo, :, cols], rs_ss.at[t], rs_rs.at[t], device).start()

        pltpu.make_async_copy(rs_s.at[lo, :, cols], rs_r.at[lo, :, cols], rs_rs.at[t]).start()

    def back_input(t):
        k = ORDER[t]
        w = 128 * (k + 1)
        for quarter in range(4):
            cols = slice(quarter * CW, (quarter + 1) * CW)
            g = g_r[k, quarter * 8:(quarter + 1) * 8].reshape(128, CW)
            v = dot_nn(inner_t[:w, k * 128:(k + 1) * 128], g)
            if t > 0:
                v = v + ig_acc[:w, cols]
            ig_out[k * 128:w, cols] = v[k * 128:].astype(BF)
            if k > 0:
                ig_acc[:k * 128, cols] = v[:k * 128]
        ig_copy(t).start()

    def gather(t):
        k = ORDER[t]
        w = 128 * (k + 1)
        cols = slice(OFFS[k], OFFS[k] + w)
        wait_bytes(rs_r.at[:, :, cols], rs_rs.at[t])
        total = rs_r[0, :, cols].astype(F32)
        for i in range(1, 8):
            total = total + rs_r[i, :, cols].astype(F32)
        ag[lo, :, cols] = total.astype(BF)

        @pl.loop(1, 8)
        def _(i):
            remote(ag.at[lo, :, cols], ag.at[lo, :, cols], ag_ss.at[t], ag_rs.at[t], dp_peer(i)[1]).start()

    def ig_copy(t):
        rows = pl.ds(ORDER[t] * 128, 128)
        return pltpu.make_async_copy(ig_out.at[rows], ig_res.at[rows], out_sem.at[t])

    def ag_copy(t):
        cols = slice(OFFS[ORDER[t]], OFFS[ORDER[t]] + 128 * (ORDER[t] + 1))
        return pltpu.make_async_copy(ag.at[:, :, cols], ag_res.at[:, :, cols], out_sem.at[NI + t])

    def inner_result(t):
        cols = slice(OFFS[ORDER[t]], OFFS[ORDER[t]] + 128 * (ORDER[t] + 1))
        wait_bytes(ag.at[pl.ds(0, 7), :, cols], ag_rs.at[t])
        ag_copy(t).start()

    @pl.when(h == 1)
    def _():
        blk[:, :8] = jnp.zeros((NI, 8, PP, CW), BF)


    outer_pass()
    outer_wait()
    for t in range(NI):
        build(ORDER[t])
    for t in range(NI - 1):
        mix(t)
        outer_part(t)
        back(t)
        back_input(t)
        if t == 2:
            gather(0)

    mix(3)
    outer_part(3)
    back(3)

    for a in range(4):
        src = lax.rem(y + a, 4)
        wait_bytes(sy_r.at[src], sy_rs.at[src])
    v = sy_r[0].astype(F32) + sy_r[1].astype(F32) + sy_r[2].astype(F32) + sy_r[3].astype(F32)
    ss_s[...] = v.astype(BF).reshape(8, 32, 128)

    @pl.loop(1, 8)
    def _(i):
        to, device = dp_peer(i)
        remote(ss_s.at[to], ss_r.at[lo], ss_sem.at[0], ss_sem.at[1], device).start()

    pltpu.make_async_copy(ss_s.at[lo], ss_r.at[lo], ss_sem.at[1]).start()

    gather(1)
    gather(2)
    back_input(3)
    inner_result(0)
    gather(3)

    wait_bytes(ss_r, ss_sem.at[1])
    total = ss_r[0].astype(F32)
    for i in range(1, 8):
        total = total + ss_r[i].astype(F32)
    sg[zme] = total.astype(BF)

    @pl.loop(1, NZ)
    def _(i):
        remote(sg.at[zme], sg.at[zme], sg_sem.at[0], sg_sem.at[1], ring_peer(i)[1]).start()

    inner_result(1)
    inner_result(2)

    wait_bytes(sg.at[pl.ds(0, NZ - 1)], sg_sem.at[1])
    sg_copy = pltpu.make_async_copy(sg, sg_res, out_sem.at[2 * NI])
    sg_copy.start()
    inner_result(3)

    sg_copy.wait()
    for t in range(NI):
        ig_copy(t).wait()
        ag_copy(t).wait()

    for t in range(NI):
        cols = slice(OFFS[ORDER[t]], OFFS[ORDER[t]] + 128 * (ORDER[t] + 1))
        wait_bytes(cot_s.at[t, pl.ds(0, PD - 1)], c_ss.at[t])
        wait_bytes(g_s.at[t, pl.ds(0, PD - 1)], g_ss.at[t])
        @pl.when(h == 1)
        def _():
            cross(t, 0).wait_send()

        for part in range(1, PARTS):
            cross(t, part).wait_send()
        wait_bytes(rs_s.at[pl.ds(0, 7), :, cols], rs_ss.at[t])
        wait_bytes(ag.at[pl.ds(0, 7), :, cols], ag_ss.at[t])

        @pl.when(y != t)
        def _():
            wait_bytes(sy_s.at[t], sy_ss.at[t])

    for a in range(7):
        wait_bytes(ot, o_ss.at[a])
    wait_bytes(x_s.at[pl.ds(0, PD - 1)], x_sem.at[0])
    wait_bytes(ss_s.at[pl.ds(0, 7)], ss_sem.at[0])
    wait_bytes(sg.at[pl.ds(0, NZ - 1)], sg_sem.at[0])


def results_kernel(
    ig_in, ag_in, sg_in, ig_out, inner_out, outer_out, ig, ag, sg, inner, spread, outer, sem
):
    h = coords()[2]
    scale = 1.0 / math.sqrt(8192.0)
    load_ag = pltpu.make_async_copy(ag_in, ag, sem.at[1])
    load_ag.start()
    load_sg = pltpu.make_async_copy(sg_in, sg, sem.at[2])
    load_sg.start()
    load_ig = pltpu.make_async_copy(ig_in, ig, sem.at[0])
    load_ig.start()

    load_ag.wait()
    stores = []
    for k in range(NI):
        w = 128 * (k + 1)
        v = ag[:, :, OFFS[k]:OFFS[k] + w].astype(F32)
        for hh in range(2):
            start = k * 128 + hh * 64
            part = v[:, 8 * hh:8 * hh + 8, :].reshape(64, w) * scale
            keep = iota((64, w), 0) + start >= iota((64, w), 1)
            inner[start:start + 64, :w] = jnp.where(keep, part, 0.0)
            if w < B:
                inner[start:start + 64, w:] = jnp.zeros((64, B - w), F32)
        rows = pl.ds(k * 128, 128)
        stores.append(pltpu.make_async_copy(inner.at[rows], inner_out.at[rows], sem.at[3 + k]))
        stores[-1].start()

    load_ig.wait()
    whole = pltpu.make_async_copy(ig, ig_out, sem.at[4 + NI])
    whole.start()
    load_sg.wait()
    parts = []
    for hs in range(2):
        v = sg[hs * 8:(hs + 1) * 8].astype(F32).reshape(16, 16, 128)
        v = jnp.where(h == 0, v[:, :8], v[:, 8:])
        parts.append(v.reshape(128, 128).astype(BF))
    c_r = iota((128, 128), 0)
    c_c = iota((128, 128), 1)
    for bh in range(4):
        v = jnp.zeros((128, 128), F32)
        for hs in range(2):
            el = c_r - 32 * bh
            col = (el >= 0) & (el < 32) & (c_c == 16 * (el // 8) + 8 * hs + lax.rem(el, 8))
            v = v + dot_nn(parts[hs], col.astype(BF))
        for g in range(2):
            base = 32 * (bh % 2) + 16 * g + 8 * (bh // 2)
            keep = iota((64, 128), 0) // 8 + base >= iota((64, 128), 1)
            spread[base * 8:base * 8 + 64] = jnp.where(keep, v[64 * g:64 * g + 64] * scale, 0.0)
    for t in range(8):
        outer[t] = spread[pl.ds(t, 64, stride=8), :][:, :64]
    last = pltpu.make_async_copy(outer, outer_out, sem.at[3 + NI])
    last.start()
    whole.wait()
    for store in stores:
        store.wait()
    last.wait()


def local(activations, cotangent, inner_weight, outer_weight):
    vmem = pl.BlockSpec(memory_space=pltpu.VMEM)
    dma = pltpu.SemaphoreType.DMA
    scratch = [
        pltpu.VMEM((B, D), BF),
        pltpu.VMEM((B, D), BF),
        pltpu.VMEM((B, B), BF),
        pltpu.VMEM((8, 64, 64), BF),
        pltpu.VMEM((NI, PD, PP, CW), BF),
        pltpu.VMEM((NI, 2 * PD, PP, CW), BF),
        pltpu.VMEM((NI, PD, PP, CW), BF),
        pltpu.VMEM((NI, PD, PP, CW), BF),
        pltpu.VMEM((PD, NI, PP, CW), BF),
        pltpu.VMEM((PD, NI, PP, CW), BF),
        pltpu.VMEM((B, B), BF),
        pltpu.VMEM((B, B), BF),
        pltpu.VMEM((256, 128), F32),
        pltpu.VMEM((256, 128), BF),
        pltpu.VMEM((NI, 2, 256, 128), BF),
        pltpu.VMEM((NI, 512, 1024), BF),
        pltpu.VMEM((B, D), BF),
        pltpu.VMEM((B, D), F32),
        pltpu.VMEM((8, 16, PACK), BF),
        pltpu.VMEM((8, 16, PACK), BF),
        pltpu.VMEM((8, 16, PACK), BF),
        pltpu.VMEM((NI, 256, 128), BF),
        pltpu.VMEM((NI, 256, 128), BF),
        pltpu.VMEM((8, 32, 128), BF),
        pltpu.VMEM((8, 32, 128), BF),
        pltpu.VMEM((NZ, 32, 128), BF),
        dma((4,)),
        dma((NI,)), dma((NI,)),
        dma((NI, PARTS)), dma((NI, PARTS)),
        dma((2,)),
        dma((NI,)), dma((NI,)),
        dma((7,)), dma((8,)),
        dma((NI,)), dma((NI,)), dma((NI,)), dma((NI,)),
        dma((NI,)), dma((NI,)),
        dma((2,)), dma((2,)),
        dma((2 * NI + 1,)),
    ]
    hbm = pl.BlockSpec(memory_space=pltpu.HBM)
    sums = pl.pallas_call(
        kernel,
        out_shape=(
            jax.ShapeDtypeStruct((B, D), BF),
            jax.ShapeDtypeStruct((8, 16, PACK), BF),
            jax.ShapeDtypeStruct((NZ, 32, 128), BF),
        ),
        in_specs=[hbm] * 4,
        out_specs=(hbm, hbm, hbm),
        scratch_shapes=scratch,
        compiler_params=pltpu.CompilerParams(
            collective_id=0, has_side_effects=True, vmem_limit_bytes=62 * 1024 * 1024
        ),
        cost_estimate=pl.CostEstimate(flops=8_000_000_000, bytes_accessed=6_000_000, transcendentals=0),
        name="mixer",
    )(activations[0, 0], cotangent[0, 0], inner_weight[0], outer_weight)
    ig, inner_grad, outer_grad = pl.pallas_call(
        results_kernel,
        out_shape=(
            jax.ShapeDtypeStruct((B, D), BF),
            jax.ShapeDtypeStruct((B, B), F32),
            jax.ShapeDtypeStruct((8, 64, 64), F32),
        ),
        in_specs=[hbm] * 3,
        out_specs=(hbm, hbm, hbm),
        scratch_shapes=[
            pltpu.VMEM((B, D), BF),
            pltpu.VMEM((8, 16, PACK), BF),
            pltpu.VMEM((NZ, 32, 128), BF),
            pltpu.VMEM((B, B), F32),
            pltpu.VMEM((512, 128), F32),
            pltpu.VMEM((8, 64, 64), F32),
            dma((5 + NI,)),
        ],
        compiler_params=pltpu.CompilerParams(vmem_limit_bytes=62 * 1024 * 1024),
        cost_estimate=pl.CostEstimate(flops=50_000_000, bytes_accessed=5_000_000, transcendentals=0),
        name="results",
    )(*sums)
    return ig[None, None], inner_grad[None], outer_grad


def solution(mesh):
    placed = (
        P("dp", "seq", None, None),
        P("dp", "seq", None, None),
        P("seq", None, None),
        P("seq", None, None),
    )
    return jax.shard_map(
        local,
        mesh=mesh,
        in_specs=placed,
        out_specs=(P("dp", "seq", None, None), P("seq", None, None), P("seq", None, None)),
        check_vma=False,
    )
```

```python
import functools
import math

import jax
import jax.numpy as jnp
from jax import lax
from jax.experimental import pallas as pl
from jax.experimental.pallas import tpu as pltpu
from jax.sharding import PartitionSpec as P

MESH = pl.DeviceIdType.MESH
BF = jnp.bfloat16
F32 = jnp.float32

B = 512
D = 1024
NI = 4
CW = D // NI
PD = 32
PP = 16
NZ = 16
OFFS = (0, 128, 384, 768)
ORDER = (3, 2, 1, 0)
TWO = (0, 1)
PARTS = 4
PACK = 1280


def coords():
    lo = lax.axis_index("dp")
    s = lax.axis_index("seq")
    core = lax.rem(s, 2)
    x = lax.rem(s // 2, 4)
    h = lax.rem(s // 8, 2)
    y = s // 16
    return lo, y, h, x, core


def plane_peers():
    lo, y, h, x, core = coords()
    offs = []
    for b in range(4):
        for c in range(2):
            offs.append(lax.rem(x + b, 4) * 2 + lax.rem(core + c, 2))

    def row(a):
        py = lax.rem(y + a, 4)
        return py * 8, py * 16 + h * 8

    return row, offs, lo


def ring_peer(i):
    lo, y, h, x, core = coords()
    z = lax.rem(h * 8 + lo + i, NZ)
    return z, (lax.rem(z, 8), y * 16 + (z // 8) * 8 + x * 2 + core)


def dp_peer(i):
    lo, y, h, x, core = coords()
    t = lax.rem(lo + i, 8)
    return t, (t, y * 16 + h * 8 + x * 2 + core)


def remote(src, dst, send, recv, device):
    return pltpu.make_async_remote_copy(
        src_ref=src, dst_ref=dst, send_sem=send, recv_sem=recv, device_id=device, device_id_type=MESH
    )


def wait_bytes(ref, sem):
    pltpu.make_async_copy(ref, ref, sem).wait()


def iota(shape, dim):
    return lax.broadcasted_iota(jnp.int32, shape, dim)


def dot_nt(a, b):
    return lax.dot_general(a, b, (((1,), (1,)), ((), ())), preferred_element_type=F32)


def dot_nn(a, b):
    return lax.dot_general(a, b, (((1,), (0,)), ((), ())), preferred_element_type=F32)


def dot_tn(a, b):
    return lax.dot_general(a, b, (((0,), (0,)), ((), ())), preferred_element_type=F32)


def halves(a, b):
    first = jnp.concatenate([a[:8], b[:8]], axis=0)
    second = jnp.concatenate([a[8:], b[8:]], axis=0)
    return first.astype(BF), second.astype(BF)


def kernel(
    act_in, cot_in, inner_in, outer_in, ig_res, ag_res, sg_res,
    act, cot, inner, outer, cot_s, blk, g_s, g_r, x_s, x_r, inner_p, inner_t,
    oscr, ot, ow, wmat, ig_out, ig_acc, rs_s, rs_r, ag, sy_s, sy_r, ss_s, ss_r, sh, sg,
    in_sem, c_ss, c_rs, z_ss, z_rs, x_sem, g_ss, g_rs, o_ss, o_rs, rs_ss, rs_rs, ag_ss, ag_rs, agp_rs, agf_rs,
    sy_ss, sy_rs, ss_sem, sg_sem, out_sem,
):
    lo, y, h, x, core = coords()
    me = y * 8 + x * 2 + core
    zme = h * 8 + lo
    peer_row, peer_offs, _ = plane_peers()
    mine = h * PD
    other = (1 - h) * PD

    def column_peer(a):
        py = lax.rem(y + a, 4)
        return py, (lo, py * 16 + h * 8 + x * 2 + core)

    loads = [
        pltpu.make_async_copy(a, b, in_sem.at[n])
        for n, (a, b) in enumerate(((cot_in, cot), (outer_in, outer), (inner_in, inner), (act_in, act)))
    ]
    for load in loads:
        load.start()

    barrier = pltpu.get_barrier_semaphore()

    @pl.loop(1, NZ)
    def _(i):
        pl.semaphore_signal(barrier, inc=1, device_id=ring_peer(i)[1], device_id_type=MESH)

    def plane_loop(body):
        @pl.loop(0, 4)
        def _(a):
            place, seq = peer_row(a)
            for off in peer_offs[1:]:
                body(place + off, (lo, seq + off))

        @pl.loop(1, 4)
        def _(a):
            place, seq = peer_row(a)
            body(place + peer_offs[0], (lo, seq + peer_offs[0]))

    plane_loop(lambda d, device: pl.semaphore_signal(barrier, inc=1, device_id=device, device_id_type=MESH))

    loads[0].wait()

    @pl.loop(0, 16)
    def _(q):
        big, u = q // 4, lax.rem(q, 4)
        at = pl.multiple_of(big * 128 + u * 16, 16)
        a = cot[pl.ds(at, 16), :].astype(F32)
        b = cot[pl.ds(at + 64, 16), :].astype(F32)
        first, second = halves(a, b)
        for quarter in range(4):
            cols = slice(quarter * CW, (quarter + 1) * CW)
            cot_s[big, quarter * 8 + u * 2] = first[:, cols]
            cot_s[big, quarter * 8 + u * 2 + 1] = second[:, cols]

    loads[1].wait()
    low = iota((64, 64), 0) >= iota((64, 64), 1)
    for t in range(8):
        v = jnp.where(low, outer[t].astype(F32), 0.0)
        oscr[pl.ds(t, 32, stride=8), :] = jnp.concatenate([v[:32], v[32:]], axis=1)
    ot[...] = oscr[...].astype(BF)

    pl.semaphore_wait(barrier, PD - 1 + NZ - 1)

    def a2a_start(src, dst, send, recv):
        plane_loop(lambda d, device: remote(src(d), dst(me), send, recv, device).start())
        pltpu.make_async_copy(src(me), dst(me), recv).start()

    def cross(t, part):
        size = PD // PARTS
        rows = blk.at[ORDER[t], pl.ds(mine + part * size, size)]
        return remote(rows, rows, z_ss.at[t, part], z_rs.at[t, part], ring_peer(8)[1])

    def cross_wait(t):
        size = PD // PARTS
        @pl.when(h == 0)
        def _():
            wait_bytes(blk.at[ORDER[t], pl.ds(other, size)], z_rs.at[t, 0])

        for part in range(1, PARTS):
            wait_bytes(blk.at[ORDER[t], pl.ds(other + part * size, size)], z_rs.at[t, part])

    def own_start(t):
        k = ORDER[t]
        a2a_start(lambda d: cot_s.at[k, d], lambda d: blk.at[k, mine + d], c_ss.at[t], c_rs.at[t, y])

    def cross_when_here(t):
        size = PD // PARTS
        for a in range(PARTS):
            part = lax.rem(y + PARTS - a, PARTS)
            wait_bytes(blk.at[ORDER[t], pl.ds(mine + part * size, size)], c_rs.at[t, part])

            @pl.when(jnp.logical_or(h == 1, part > 0))
            def _():
                cross(t, part).start()

    own_start(0)
    for a in range(1, 4):
        remote(ot, ow.at[y, h], o_ss.at[a], o_rs.at[a], column_peer(a)[1]).start()
    remote(ot, ow.at[y, h], o_ss.at[0], o_rs.at[0], ring_peer(8)[1]).start()
    own_copy = pltpu.make_async_copy(ot, ow.at[y, h], o_rs.at[7])
    own_copy.start()
    cross_when_here(0)
    own_start(1)
    own_start(2)
    cross_when_here(1)
    own_start(3)
    cross_when_here(2)
    cross_when_here(3)

    loads[2].wait()

    @pl.loop(0, 16)
    def _(q):
        big, u = q // 4, lax.rem(q, 4)
        at = pl.multiple_of(big * 128 + u * 16, 16)

        def rows(start):
            v = inner[pl.ds(start, 16), :].astype(F32)
            return jnp.where(iota((16, B), 0) + start >= iota((16, B), 1), v, 0.0)

        first, second = halves(rows(at), rows(at + 64))
        to = pl.multiple_of(big * 128 + u * 32, 32)
        inner_p[pl.ds(to, 16), :] = first
        inner_p[pl.ds(to + 16, 16), :] = second

    inner_t[...] = inner_p[...].T
    loads[3].wait()

    @pl.loop(0, 4)
    def _(q):
        rows = pl.ds(pl.multiple_of(q * 128, 128), 128)
        v = dot_nn(inner_p[rows, :], act[...]).astype(BF)
        for quarter in range(4):
            cols = slice(quarter * CW, (quarter + 1) * CW)
            x_s[quarter * 8:(quarter + 1) * 8, q] = v[:, cols].reshape(8, PP, CW)

    a2a_start(lambda d: x_s.at[d], lambda d: x_r.at[d], x_sem.at[0], x_sem.at[1])

    def outer_pass():
        wait_bytes(ow.at[y, 1 - h], o_rs.at[0])
        for a in range(1, 4):
            remote(ow.at[y, 1 - h], ow.at[y, 1 - h], o_ss.at[3 + a], o_rs.at[3 + a], column_peer(a)[1]).start()

    def outer_wait():
        own_copy.wait()
        for a in range(1, 4):
            src = lax.rem(y + 4 - a, 4)
            wait_bytes(ow.at[src, h], o_rs.at[a])
            wait_bytes(ow.at[src, 1 - h], o_rs.at[3 + a])

    def build(k):
        el = iota((64, 512), 1) // 16
        pick = (iota((64, 512), 0) == 16 * (el // 8) + 8 * h + lax.rem(el, 8)).astype(BF)
        same = lax.rem(iota((128, 512), 0), 16) == lax.rem(iota((128, 512), 1), 16)

        @pl.loop(0, 8)
        def _(g):
            group = 2 * lax.rem(g, 4) + g // 4
            rows = pl.ds(pl.multiple_of(lax.rem(group, 4) * 64, 64), 64)
            both = []
            for hh in range(2):
                v = ow[k, hh, rows, :].astype(F32)
                both.append(jnp.where(group < 4, v[:, :64], v[:, 64:]).reshape(8, 8, 64))
            v = jnp.concatenate(both, axis=1).reshape(128, 64).astype(BF)
            w = jnp.where(same, dot_nn(v, pick), 0.0).astype(BF)
            wmat[k, :, pl.ds(pl.multiple_of(g * 128, 128), 128)] = w.T

    def mix(t):
        k = ORDER[t]
        cross_wait(t)

        @pl.loop(0, 4)
        def _(a):
            place, seq = peer_row(a)
            rows = pl.ds(pl.multiple_of(place * PP, 128), 128)
            v = dot_nn(wmat[k, rows, :], blk[k].reshape(1024, CW)).astype(BF)
            g_s[k, pl.ds(place, 8)] = v.reshape(8, PP, CW)

            def give(off):
                remote(
                    g_s.at[k, place + off], g_r.at[k, me], g_ss.at[t], g_rs.at[t], (lo, seq + off)
                ).start()

            for off in peer_offs[1:]:
                give(off)

            @pl.when(a > 0)
            def _():
                give(peer_offs[0])

        pltpu.make_async_copy(g_s.at[k, me], g_r.at[k, me], g_rs.at[t]).start()

    def outer_part(t):
        k = ORDER[t]
        if t == 0:
            wait_bytes(x_r, x_sem.at[1])
        same = lax.rem(iota((128, 512), 0), 16) == lax.rem(iota((128, 512), 1), 16)

        @pl.loop(0, 2)
        def _(half):
            total = jnp.zeros((128, 128), F32)
            for bh in range(4):
                v = dot_nt(blk[k, pl.ds(bh * 16 + half * 8, 8)].reshape(128, CW), x_r[:, k].reshape(512, CW))
                put = (iota((512, 128), 1) == 32 * bh + iota((512, 128), 0) // 16).astype(BF)
                total = total + dot_nn(jnp.where(same, v, 0.0).astype(BF), put)
            sy_s[k, pl.ds(pl.multiple_of(half * 128, 128), 128), :] = total.astype(BF)

        @pl.when(y == k)
        def _():
            pltpu.make_async_copy(sy_s.at[k], sy_r.at[y], sy_rs.at[y]).start()

        @pl.when(y != k)
        def _():
            device = (lo, k * 16 + h * 8 + x * 2 + core)
            remote(sy_s.at[k], sy_r.at[y], sy_ss.at[k], sy_rs.at[y], device).start()

    def back(t):
        k = ORDER[t]
        w = 128 * (k + 1)
        wait_bytes(g_r.at[k], g_rs.at[t])
        v = jnp.zeros((128, w), F32)
        for quarter in range(4):
            cols = slice(quarter * CW, (quarter + 1) * CW)
            v = v + dot_nt(g_r[k, quarter * 8:(quarter + 1) * 8].reshape(128, CW), act[:w, cols])
        cols = slice(OFFS[k], OFFS[k] + w)
        rs_s[:, :, cols] = v.astype(BF).reshape(8, 16, w)

        @pl.loop(1, 8)
        def _(i):
            to, device = dp_peer(i)
            remote(rs_s.at[to, :, cols], rs_r.at[lo, :, cols], rs_ss.at[t], rs_rs.at[t], device).start()

        pltpu.make_async_copy(rs_s.at[lo, :, cols], rs_r.at[lo, :, cols], rs_rs.at[t]).start()

    def back_input(t):
        k = ORDER[t]
        w = 128 * (k + 1)
        for quarter in range(4):
            cols = slice(quarter * CW, (quarter + 1) * CW)
            g = g_r[k, quarter * 8:(quarter + 1) * 8].reshape(128, CW)
            v = dot_nn(inner_t[:w, k * 128:(k + 1) * 128], g)
            if t > 0:
                v = v + ig_acc[:w, cols]
            ig_out[k * 128:w, cols] = v[k * 128:].astype(BF)
            if k > 0:
                ig_acc[:k * 128, cols] = v[:k * 128]
        ig_copy(t).start()

    def gather(t):
        k = ORDER[t]
        w = 128 * (k + 1)
        cols = slice(OFFS[k], OFFS[k] + w)
        wait_bytes(rs_r.at[:, :, cols], rs_rs.at[t])
        total = rs_r[0, :, cols].astype(F32)
        for i in range(1, 8):
            total = total + rs_r[i, :, cols].astype(F32)
        ag[lo, :, cols] = total.astype(BF)

        if t in TWO:
            for i in range(4):
                own = ag.at[lo, :, cols]
                device = half_peer(i)[1] if i else dp_peer(4)[1]
                remote(own, own, ag_ss.at[t], ag_rs.at[t] if i else agp_rs.at[t], device).start()
            return

        @pl.loop(1, 8)
        def _(i):
            remote(ag.at[lo, :, cols], ag.at[lo, :, cols], ag_ss.at[t], ag_rs.at[t], dp_peer(i)[1]).start()

    def half_peer(i):
        to = (lo // 4) * 4 + lax.rem(lo + i, 4)
        return to, (to, y * 16 + h * 8 + x * 2 + core)

    def forward(t):
        cols = slice(OFFS[ORDER[t]], OFFS[ORDER[t]] + 128 * (ORDER[t] + 1))
        theirs = ag.at[dp_peer(4)[0], :, cols]
        wait_bytes(theirs, agp_rs.at[t])
        for i in range(1, 4):
            remote(theirs, theirs, ag_ss.at[t], agf_rs.at[t], half_peer(i)[1]).start()

    def ig_copy(t):
        rows = pl.ds(ORDER[t] * 128, 128)
        return pltpu.make_async_copy(ig_out.at[rows], ig_res.at[rows], out_sem.at[t])

    def ag_copy(t):
        cols = slice(OFFS[ORDER[t]], OFFS[ORDER[t]] + 128 * (ORDER[t] + 1))
        return pltpu.make_async_copy(ag.at[:, :, cols], ag_res.at[:, :, cols], out_sem.at[NI + t])

    def inner_result(t):
        cols = slice(OFFS[ORDER[t]], OFFS[ORDER[t]] + 128 * (ORDER[t] + 1))
        if t in TWO:
            wait_bytes(ag.at[pl.ds(0, 3), :, cols], ag_rs.at[t])
            wait_bytes(ag.at[pl.ds(0, 3), :, cols], agf_rs.at[t])
        else:
            wait_bytes(ag.at[pl.ds(0, 7), :, cols], ag_rs.at[t])
        ag_copy(t).start()

    @pl.when(h == 1)
    def _():
        blk[:, :8] = jnp.zeros((NI, 8, PP, CW), BF)


    outer_pass()
    outer_wait()
    for t in range(NI):
        build(ORDER[t])
    for t in range(NI - 1):
        mix(t)
        outer_part(t)
        back(t)
        back_input(t)
        if t == 2:
            gather(0)

    mix(3)
    outer_part(3)
    forward(0)
    back(3)

    for a in range(4):
        src = lax.rem(y + a, 4)
        wait_bytes(sy_r.at[src], sy_rs.at[src])
    v = sy_r[0].astype(F32) + sy_r[1].astype(F32) + sy_r[2].astype(F32) + sy_r[3].astype(F32)
    ss_s[...] = v.astype(BF).reshape(8, 32, 128)

    @pl.loop(1, 8)
    def _(i):
        to, device = dp_peer(i)
        remote(ss_s.at[to], ss_r.at[lo], ss_sem.at[0], ss_sem.at[1], device).start()

    pltpu.make_async_copy(ss_s.at[lo], ss_r.at[lo], ss_sem.at[1]).start()

    gather(1)
    gather(2)
    back_input(3)
    inner_result(0)
    gather(3)
    forward(1)

    wait_bytes(ss_r, ss_sem.at[1])
    total = ss_r[0].astype(F32)
    for i in range(1, 8):
        total = total + ss_r[i].astype(F32)
    for hh in range(2):
        sh[hh] = jnp.concatenate([total[8 * hh:8 * hh + 8], total[16 + 8 * hh:24 + 8 * hh]], axis=0).astype(BF)
    sg[zme] = sh[h]

    @pl.loop(1, NZ)
    def _(i):
        z, device = ring_peer(i)
        remote(sh.at[z // 8], sg.at[zme], sg_sem.at[0], sg_sem.at[1], device).start()

    inner_result(1)
    inner_result(2)

    wait_bytes(sg.at[pl.ds(0, NZ - 1)], sg_sem.at[1])
    sg_copy = pltpu.make_async_copy(sg, sg_res, out_sem.at[2 * NI])
    sg_copy.start()
    inner_result(3)

    sg_copy.wait()
    for t in range(NI):
        ig_copy(t).wait()
        ag_copy(t).wait()

    for t in range(NI):
        cols = slice(OFFS[ORDER[t]], OFFS[ORDER[t]] + 128 * (ORDER[t] + 1))
        wait_bytes(cot_s.at[t, pl.ds(0, PD - 1)], c_ss.at[t])
        wait_bytes(g_s.at[t, pl.ds(0, PD - 1)], g_ss.at[t])
        @pl.when(h == 1)
        def _():
            cross(t, 0).wait_send()

        for part in range(1, PARTS):
            cross(t, part).wait_send()
        wait_bytes(rs_s.at[pl.ds(0, 7), :, cols], rs_ss.at[t])
        wait_bytes(ag.at[pl.ds(0, 7), :, cols], ag_ss.at[t])

        @pl.when(y != t)
        def _():
            wait_bytes(sy_s.at[t], sy_ss.at[t])

    for a in range(7):
        wait_bytes(ot, o_ss.at[a])
    wait_bytes(x_s.at[pl.ds(0, PD - 1)], x_sem.at[0])
    wait_bytes(ss_s.at[pl.ds(0, 7)], ss_sem.at[0])
    wait_bytes(sg.at[pl.ds(0, NZ - 1)], sg_sem.at[0])


def results_kernel(
    ig_in, ag_in, sg_in, ig_out, inner_out, outer_out, ig, ag, sg, inner, spread, outer, sem
):
    scale = 1.0 / math.sqrt(8192.0)
    load_ag = pltpu.make_async_copy(ag_in, ag, sem.at[1])
    load_ag.start()
    load_sg = pltpu.make_async_copy(sg_in, sg, sem.at[2])
    load_sg.start()
    loads, wholes = [], []
    for k in range(NI):
        rows = pl.ds(k * 128, 128)
        loads.append(pltpu.make_async_copy(ig_in.at[rows], ig.at[rows], sem.at[4 + NI + k]))
        wholes.append(pltpu.make_async_copy(ig.at[rows], ig_out.at[rows], sem.at[4 + 2 * NI + k]))
        loads[-1].start()

    load_ag.wait()
    stores = []
    for k in range(NI):
        w = 128 * (k + 1)
        v = ag[:, :, OFFS[k]:OFFS[k] + w].astype(F32)
        for hh in range(2):
            start = k * 128 + hh * 64
            part = v[:, 8 * hh:8 * hh + 8, :].reshape(64, w) * scale
            keep = iota((64, w), 0) + start >= iota((64, w), 1)
            inner[start:start + 64, :w] = jnp.where(keep, part, 0.0)
            if w < B:
                inner[start:start + 64, w:] = jnp.zeros((64, B - w), F32)
        rows = pl.ds(k * 128, 128)
        stores.append(pltpu.make_async_copy(inner.at[rows], inner_out.at[rows], sem.at[3 + k]))
        stores[-1].start()
        loads[k].wait()
        wholes[k].start()

    load_sg.wait()
    parts = []
    for hs in range(2):
        parts.append(sg[hs * 8:(hs + 1) * 8].reshape(128, 128))
    c_r = iota((128, 128), 0)
    c_c = iota((128, 128), 1)
    for bh in range(4):
        v = jnp.zeros((128, 128), F32)
        for hs in range(2):
            el = c_r - 32 * bh
            col = (el >= 0) & (el < 32) & (c_c == 16 * (el // 8) + 8 * hs + lax.rem(el, 8))
            v = v + dot_nn(parts[hs], col.astype(BF))
        for g in range(2):
            base = 32 * (bh % 2) + 16 * g + 8 * (bh // 2)
            keep = iota((64, 128), 0) // 8 + base >= iota((64, 128), 1)
            spread[base * 8:base * 8 + 64] = jnp.where(keep, v[64 * g:64 * g + 64] * scale, 0.0)
    for t in range(8):
        outer[t] = spread[pl.ds(t, 64, stride=8), :][:, :64]
    last = pltpu.make_async_copy(outer, outer_out, sem.at[3 + NI])
    last.start()
    for store in stores + wholes:
        store.wait()
    last.wait()


def local(activations, cotangent, inner_weight, outer_weight):
    vmem = pl.BlockSpec(memory_space=pltpu.VMEM)
    dma = pltpu.SemaphoreType.DMA
    scratch = [
        pltpu.VMEM((B, D), BF),
        pltpu.VMEM((B, D), BF),
        pltpu.VMEM((B, B), BF),
        pltpu.VMEM((8, 64, 64), BF),
        pltpu.VMEM((NI, PD, PP, CW), BF),
        pltpu.VMEM((NI, 2 * PD, PP, CW), BF),
        pltpu.VMEM((NI, PD, PP, CW), BF),
        pltpu.VMEM((NI, PD, PP, CW), BF),
        pltpu.VMEM((PD, NI, PP, CW), BF),
        pltpu.VMEM((PD, NI, PP, CW), BF),
        pltpu.VMEM((B, B), BF),
        pltpu.VMEM((B, B), BF),
        pltpu.VMEM((256, 128), F32),
        pltpu.VMEM((256, 128), BF),
        pltpu.VMEM((NI, 2, 256, 128), BF),
        pltpu.VMEM((NI, 512, 1024), BF),
        pltpu.VMEM((B, D), BF),
        pltpu.VMEM((B, D), F32),
        pltpu.VMEM((8, 16, PACK), BF),
        pltpu.VMEM((8, 16, PACK), BF),
        pltpu.VMEM((8, 16, PACK), BF),
        pltpu.VMEM((NI, 256, 128), BF),
        pltpu.VMEM((NI, 256, 128), BF),
        pltpu.VMEM((8, 32, 128), BF),
        pltpu.VMEM((8, 32, 128), BF),
        pltpu.VMEM((2, 16, 128), BF),
        pltpu.VMEM((NZ, 16, 128), BF),
        dma((4,)),
        dma((NI,)), dma((NI, PARTS)),
        dma((NI, PARTS)), dma((NI, PARTS)),
        dma((2,)),
        dma((NI,)), dma((NI,)),
        dma((7,)), dma((8,)),
        dma((NI,)), dma((NI,)), dma((NI,)), dma((NI,)), dma((NI,)), dma((NI,)),
        dma((NI,)), dma((NI,)),
        dma((2,)), dma((2,)),
        dma((2 * NI + 1,)),
    ]
    hbm = pl.BlockSpec(memory_space=pltpu.HBM)
    sums = pl.pallas_call(
        kernel,
        out_shape=(
            jax.ShapeDtypeStruct((B, D), BF),
            jax.ShapeDtypeStruct((8, 16, PACK), BF),
            jax.ShapeDtypeStruct((NZ, 16, 128), BF),
        ),
        in_specs=[hbm] * 4,
        out_specs=(hbm, hbm, hbm),
        scratch_shapes=scratch,
        compiler_params=pltpu.CompilerParams(
            collective_id=0, has_side_effects=True, vmem_limit_bytes=62 * 1024 * 1024
        ),
        cost_estimate=pl.CostEstimate(flops=8_000_000_000, bytes_accessed=6_000_000, transcendentals=0),
        name="mixer",
    )(activations[0, 0], cotangent[0, 0], inner_weight[0], outer_weight)
    ig, inner_grad, outer_grad = pl.pallas_call(
        results_kernel,
        out_shape=(
            jax.ShapeDtypeStruct((B, D), BF),
            jax.ShapeDtypeStruct((B, B), F32),
            jax.ShapeDtypeStruct((8, 64, 64), F32),
        ),
        in_specs=[hbm] * 3,
        out_specs=(hbm, hbm, hbm),
        scratch_shapes=[
            pltpu.VMEM((B, D), BF),
            pltpu.VMEM((8, 16, PACK), BF),
            pltpu.VMEM((NZ, 16, 128), BF),
            pltpu.VMEM((B, B), F32),
            pltpu.VMEM((512, 128), F32),
            pltpu.VMEM((8, 64, 64), F32),
            dma((4 + 3 * NI,)),
        ],
        compiler_params=pltpu.CompilerParams(vmem_limit_bytes=62 * 1024 * 1024),
        cost_estimate=pl.CostEstimate(flops=50_000_000, bytes_accessed=5_000_000, transcendentals=0),
        name="results",
    )(*sums)
    return ig[None, None], inner_grad[None], outer_grad


def solution(mesh):
    placed = (
        P("dp", "seq", None, None),
        P("dp", "seq", None, None),
        P("seq", None, None),
        P("seq", None, None),
    )
    return jax.shard_map(
        local,
        mesh=mesh,
        in_specs=placed,
        out_specs=(P("dp", "seq", None, None), P("seq", None, None), P("seq", None, None)),
        check_vma=False,
    )
```

```python
import functools
import math

import jax
import jax.numpy as jnp
from jax import lax
from jax.experimental import pallas as pl
from jax.experimental.pallas import tpu as pltpu
from jax.sharding import PartitionSpec as P

MESH = pl.DeviceIdType.MESH
BF = jnp.bfloat16
F32 = jnp.float32

B = 512
D = 1024
NI = 4
CW = D // NI
PD = 32
PP = 16
NZ = 16
OFFS = (0, 128, 384, 768)
ORDER = (3, 2, 1, 0)
TWO = (0, 1)
PARTS = 4
PACK = 1280


def coords():
    lo = lax.axis_index("dp")
    s = lax.axis_index("seq")
    core = lax.rem(s, 2)
    x = lax.rem(s // 2, 4)
    h = lax.rem(s // 8, 2)
    y = s // 16
    return lo, y, h, x, core


def plane_peers():
    lo, y, h, x, core = coords()
    offs = []
    for b in range(4):
        for c in range(2):
            offs.append(lax.rem(x + b, 4) * 2 + lax.rem(core + c, 2))

    def row(a):
        py = lax.rem(y + a, 4)
        return py * 8, py * 16 + h * 8

    return row, offs, lo


def ring_peer(i):
    lo, y, h, x, core = coords()
    z = lax.rem(h * 8 + lo + i, NZ)
    return z, (lax.rem(z, 8), y * 16 + (z // 8) * 8 + x * 2 + core)


def dp_peer(i):
    lo, y, h, x, core = coords()
    t = lax.rem(lo + i, 8)
    return t, (t, y * 16 + h * 8 + x * 2 + core)


def remote(src, dst, send, recv, device):
    return pltpu.make_async_remote_copy(
        src_ref=src, dst_ref=dst, send_sem=send, recv_sem=recv, device_id=device, device_id_type=MESH
    )


def wait_bytes(ref, sem):
    pltpu.make_async_copy(ref, ref, sem).wait()


def iota(shape, dim):
    return lax.broadcasted_iota(jnp.int32, shape, dim)


def dot_nt(a, b):
    return lax.dot_general(a, b, (((1,), (1,)), ((), ())), preferred_element_type=F32)


def dot_nn(a, b):
    return lax.dot_general(a, b, (((1,), (0,)), ((), ())), preferred_element_type=F32)


def dot_tn(a, b):
    return lax.dot_general(a, b, (((0,), (0,)), ((), ())), preferred_element_type=F32)


def halves(a, b):
    first = jnp.concatenate([a[:8], b[:8]], axis=0)
    second = jnp.concatenate([a[8:], b[8:]], axis=0)
    return first.astype(BF), second.astype(BF)


def kernel(
    act_in, cot_in, inner_in, outer_in, ig_res, ag_res, sg_res,
    act, cot, inner, outer, cot_s, blk, g_s, g_r, x_s, x_r, inner_p, inner_t,
    oscr, ot, ow, wmat, g_own, s_own, ig_out, ig_acc, rs_s, rs_r, ex_m, ex_s, ex_r, ag, sy_s, sy_r, ss_s, ss_r, sh, sg,
    in_sem, c_ss, c_rs, z_ss, z_rs, x_sem, g_ss, g_rs, o_ss, o_rs, rs_ss, rs_rs, ag_ss, ag_rs, agp_rs, agf_rs, ex_ss, ex_rs,
    sy_ss, sy_rs, ss_sem, sg_sem, out_sem,
):
    lo, y, h, x, core = coords()
    me = y * 8 + x * 2 + core
    zme = h * 8 + lo
    peer_row, peer_offs, _ = plane_peers()
    mine = h * PD
    other = (1 - h) * PD

    def column_peer(a):
        py = lax.rem(y + a, 4)
        return py, (lo, py * 16 + h * 8 + x * 2 + core)

    loads = [
        pltpu.make_async_copy(a, b, in_sem.at[n])
        for n, (a, b) in enumerate(((cot_in, cot), (outer_in, outer), (inner_in, inner), (act_in, act)))
    ]
    for load in loads:
        load.start()

    barrier = pltpu.get_barrier_semaphore()

    @pl.loop(1, NZ)
    def _(i):
        pl.semaphore_signal(barrier, inc=1, device_id=ring_peer(i)[1], device_id_type=MESH)

    def plane_loop(body):
        @pl.loop(0, 4)
        def _(a):
            place, seq = peer_row(a)
            for off in peer_offs[1:]:
                body(place + off, (lo, seq + off))

        @pl.loop(1, 4)
        def _(a):
            place, seq = peer_row(a)
            body(place + peer_offs[0], (lo, seq + peer_offs[0]))

    plane_loop(lambda d, device: pl.semaphore_signal(barrier, inc=1, device_id=device, device_id_type=MESH))

    loads[0].wait()

    @pl.loop(0, 16)
    def _(q):
        big, u = q // 4, lax.rem(q, 4)
        at = pl.multiple_of(big * 128 + u * 16, 16)
        a = cot[pl.ds(at, 16), :].astype(F32)
        b = cot[pl.ds(at + 64, 16), :].astype(F32)
        first, second = halves(a, b)
        for quarter in range(4):
            cols = slice(quarter * CW, (quarter + 1) * CW)
            cot_s[big, quarter * 8 + u * 2] = first[:, cols]
            cot_s[big, quarter * 8 + u * 2 + 1] = second[:, cols]

    loads[1].wait()
    keep = iota((8, 64, 64), 1) >= iota((8, 64, 64), 2)
    factors = jnp.where(keep, outer[...].astype(F32), 0.0).astype(BF)
    lane = iota((64, 128), 1)
    el = lax.rem(lane, 32)
    for side in range(2):
        total = jnp.zeros((128, 128), F32)
        for q in range(4):
            block = 16 * (el // 8) + 8 * side + lax.rem(el, 8)
            sel = ((iota((64, 128), 0) == block) & (lane // 32 == q)).astype(BF)
            total = total + dot_nn(factors[:, 16 * q:16 * q + 16].reshape(128, 64), sel)
        for t in range(8):
            oscr[pl.ds(t, 16, stride=8), :] = total[16 * t:16 * t + 16]
        ot[side] = oscr[...].astype(BF)

    pl.semaphore_wait(barrier, PD - 1 + NZ - 1)

    def a2a_start(src, dst, send, recv):
        plane_loop(lambda d, device: remote(src(d), dst(me), send, recv, device).start())
        pltpu.make_async_copy(src(me), dst(me), recv).start()

    def cross(t, part):
        size = PD // PARTS
        rows = blk.at[ORDER[t], pl.ds(mine + part * size, size)]
        return remote(rows, rows, z_ss.at[t, part], z_rs.at[t, part], ring_peer(8)[1])

    def cross_wait(t):
        size = PD // PARTS
        @pl.when(h == 0)
        def _():
            wait_bytes(blk.at[ORDER[t], pl.ds(other, size)], z_rs.at[t, 0])

        for part in range(1, PARTS):
            wait_bytes(blk.at[ORDER[t], pl.ds(other + part * size, size)], z_rs.at[t, part])

    def own_start(t):
        k = ORDER[t]
        a2a_start(lambda d: cot_s.at[k, d], lambda d: blk.at[k, mine + d], c_ss.at[t], c_rs.at[t, y])

    def cross_when_here(t):
        size = PD // PARTS
        for a in range(PARTS):
            part = lax.rem(y + PARTS - a, PARTS)
            wait_bytes(blk.at[ORDER[t], pl.ds(mine + part * size, size)], c_rs.at[t, part])

            @pl.when(jnp.logical_or(h == 1, part > 0))
            def _():
                cross(t, part).start()

    own_start(0)
    for a in range(1, 4):
        remote(ot.at[h], ow.at[y, h], o_ss.at[a], o_rs.at[a], column_peer(a)[1]).start()
    remote(ot.at[1 - h], ow.at[y, h], o_ss.at[0], o_rs.at[0], ring_peer(8)[1]).start()
    own_copy = pltpu.make_async_copy(ot.at[h], ow.at[y, h], o_rs.at[7])
    own_copy.start()
    cross_when_here(0)
    own_start(1)
    own_start(2)
    cross_when_here(1)
    own_start(3)
    cross_when_here(2)
    cross_when_here(3)

    loads[2].wait()

    @pl.loop(0, 16)
    def _(q):
        big, u = q // 4, lax.rem(q, 4)
        at = pl.multiple_of(big * 128 + u * 16, 16)

        def rows(start):
            v = inner[pl.ds(start, 16), :].astype(F32)
            return jnp.where(iota((16, B), 0) + start >= iota((16, B), 1), v, 0.0)

        first, second = halves(rows(at), rows(at + 64))
        to = pl.multiple_of(big * 128 + u * 32, 32)
        inner_p[pl.ds(to, 16), :] = first
        inner_p[pl.ds(to + 16, 16), :] = second

    inner_t[...] = inner_p[...].T
    loads[3].wait()

    @pl.loop(0, 4)
    def _(q):
        rows = pl.ds(pl.multiple_of(q * 128, 128), 128)
        v = dot_nn(inner_p[rows, :], act[...]).astype(BF)
        for quarter in range(4):
            cols = slice(quarter * CW, (quarter + 1) * CW)
            x_s[quarter * 8:(quarter + 1) * 8, q] = v[:, cols].reshape(8, PP, CW)

    a2a_start(lambda d: x_s.at[d], lambda d: x_r.at[d], x_sem.at[0], x_sem.at[1])

    def outer_pass():
        wait_bytes(ow.at[y, 1 - h], o_rs.at[0])
        for a in range(1, 4):
            remote(ow.at[y, 1 - h], ow.at[y, 1 - h], o_ss.at[3 + a], o_rs.at[3 + a], column_peer(a)[1]).start()

    def outer_wait():
        own_copy.wait()
        for a in range(1, 4):
            src = lax.rem(y + 4 - a, 4)
            wait_bytes(ow.at[src, h], o_rs.at[a])
            wait_bytes(ow.at[src, 1 - h], o_rs.at[3 + a])

    def build(k):
        lane = iota((128, 512), 0)
        el = iota((128, 512), 1) // 16
        same = lax.rem(lane, 16) == lax.rem(iota((128, 512), 1), 16)

        @pl.loop(0, 8)
        def _(g):
            group = 2 * lax.rem(g, 4) + g // 4
            rows = pl.ds(pl.multiple_of(lax.rem(group, 2) * 64, 64), 64)
            put = (lane == 32 * (group // 2) + el).astype(BF)
            both = [dot_nn(ow[k, hh, rows, :], put).reshape(8, 8, 512) for hh in range(2)]
            w = jnp.concatenate(both, axis=1).reshape(128, 512)
            wmat[k, :, pl.ds(pl.multiple_of(g * 128, 128), 128)] = jnp.where(same, w, 0.0).astype(BF).T

    theirs = pl.ds(pl.multiple_of((1 - h) * 512, 512), 512)

    def quarters(t, half, side):
        k = ORDER[t]
        same = lax.rem(iota((128, 512), 0), 16) == lax.rem(iota((128, 512), 1), 16)
        total = jnp.zeros((128, 128), F32)
        for i in range(2):
            bh = 2 * side + i
            v = dot_nt(blk[k, pl.ds(bh * 16 + half * 8, 8)].reshape(128, CW), x_r[:, k].reshape(512, CW))
            put = (iota((512, 128), 1) == 32 * bh + iota((512, 128), 0) // 16).astype(BF)
            total = total + dot_nn(jnp.where(same, v, 0.0).astype(BF), put)
        return total

    def own_products():
        t = NI - 1
        k = ORDER[t]
        ours = pl.ds(pl.multiple_of(h * 512, 512), 512)

        @pl.loop(0, 4)
        def _(q):
            rows = pl.ds(pl.multiple_of(q * 128, 128), 128)
            g_own[rows, :] = dot_nn(wmat[k, rows, ours], blk[k, pl.ds(mine, PD)].reshape(512, CW))

        @pl.loop(0, 2)
        def _(half):
            s_own[pl.ds(pl.multiple_of(half * 128, 128), 128), :] = quarters(t, half, h)

    def mix(t):
        k = ORDER[t]
        cross_wait(t)

        @pl.loop(0, 4)
        def _(a):
            place, seq = peer_row(a)
            rows = pl.ds(pl.multiple_of(place * PP, 128), 128)
            if t == NI - 1:
                v = dot_nn(wmat[k, rows, theirs], blk[k, pl.ds(other, PD)].reshape(512, CW))
                v = (v + g_own[rows, :]).astype(BF)
            else:
                v = dot_nn(wmat[k, rows, :], blk[k].reshape(1024, CW)).astype(BF)
            g_s[k, pl.ds(place, 8)] = v.reshape(8, PP, CW)

            def give(off):
                remote(
                    g_s.at[k, place + off], g_r.at[k, me], g_ss.at[t], g_rs.at[t], (lo, seq + off)
                ).start()

            for off in peer_offs[1:]:
                give(off)

            @pl.when(a > 0)
            def _():
                give(peer_offs[0])

        pltpu.make_async_copy(g_s.at[k, me], g_r.at[k, me], g_rs.at[t]).start()

    def outer_part(t):
        k = ORDER[t]
        if t == 0:
            wait_bytes(x_r, x_sem.at[1])
        @pl.loop(0, 2)
        def _(half):
            rows = pl.ds(pl.multiple_of(half * 128, 128), 128)
            if t == NI - 1:
                total = s_own[rows, :] + quarters(t, half, 1 - h)
            else:
                total = quarters(t, half, 0) + quarters(t, half, 1)
            sy_s[k, rows, :] = total.astype(BF)

        @pl.when(y == k)
        def _():
            pltpu.make_async_copy(sy_s.at[k], sy_r.at[y], sy_rs.at[y]).start()

        @pl.when(y != k)
        def _():
            device = (lo, k * 16 + h * 8 + x * 2 + core)
            remote(sy_s.at[k], sy_r.at[y], sy_ss.at[k], sy_rs.at[y], device).start()

    def back(t):
        k = ORDER[t]
        w = 128 * (k + 1)
        wait_bytes(g_r.at[k], g_rs.at[t])
        v = jnp.zeros((128, w), F32)
        for quarter in range(4):
            cols = slice(quarter * CW, (quarter + 1) * CW)
            v = v + dot_nt(g_r[k, quarter * 8:(quarter + 1) * 8].reshape(128, CW), act[:w, cols])
        cols = slice(OFFS[k], OFFS[k] + w)
        rs_s[:, :, cols] = v.astype(BF).reshape(8, 16, w)

        if t in TWO:
            at = lax.rem(lo, 4)
            for half in (0, 4):
                for i in range(1, 4):
                    to, device = half_peer(i)
                    src = rs_s.at[lax.rem(to, 4) + half, :, cols]
                    remote(src, rs_r.at[at + half, :, cols], rs_ss.at[t], rs_rs.at[t], device).start()
                pltpu.make_async_copy(
                    rs_s.at[at + half, :, cols], rs_r.at[at + half, :, cols], rs_rs.at[t]
                ).start()
            return

        @pl.loop(1, 8)
        def _(i):
            to, device = dp_peer(i)
            remote(rs_s.at[to, :, cols], rs_r.at[lo, :, cols], rs_ss.at[t], rs_rs.at[t], device).start()

        pltpu.make_async_copy(rs_s.at[lo, :, cols], rs_r.at[lo, :, cols], rs_rs.at[t]).start()

    def exchange(t):
        cols = slice(OFFS[ORDER[t]], OFFS[ORDER[t]] + 128 * (ORDER[t] + 1))
        wait_bytes(rs_r.at[:, :, cols], rs_rs.at[t])
        sums = []
        for half in (0, 4):
            total = rs_r[half, :, cols].astype(F32)
            for i in range(1, 4):
                total = total + rs_r[half + i, :, cols].astype(F32)
            sums.append(total)
        ex_m[:, cols] = jnp.where(lo < 4, sums[0], sums[1])
        ex_s[:, cols] = jnp.where(lo < 4, sums[1], sums[0]).astype(BF)
        remote(ex_s.at[:, cols], ex_r.at[:, cols], ex_ss.at[t], ex_rs.at[t], dp_peer(4)[1]).start()

    def half_peer(i):
        to = (lo // 4) * 4 + lax.rem(lo + i, 4)
        return to, (to, y * 16 + h * 8 + x * 2 + core)

    def back_input(t):
        k = ORDER[t]
        w = 128 * (k + 1)
        for quarter in range(4):
            cols = slice(quarter * CW, (quarter + 1) * CW)
            g = g_r[k, quarter * 8:(quarter + 1) * 8].reshape(128, CW)
            v = dot_nn(inner_t[:w, k * 128:(k + 1) * 128], g)
            if t > 0:
                v = v + ig_acc[:w, cols]
            ig_out[k * 128:w, cols] = v[k * 128:].astype(BF)
            if k > 0:
                ig_acc[:k * 128, cols] = v[:k * 128]
        ig_copy(t).start()

    def gather(t):
        k = ORDER[t]
        w = 128 * (k + 1)
        cols = slice(OFFS[k], OFFS[k] + w)
        if t in TWO:
            wait_bytes(ex_r.at[:, cols], ex_rs.at[t])
            total = ex_m[:, cols] + ex_r[:, cols].astype(F32)
        else:
            wait_bytes(rs_r.at[:, :, cols], rs_rs.at[t])
            total = rs_r[0, :, cols].astype(F32)
            for i in range(1, 8):
                total = total + rs_r[i, :, cols].astype(F32)
        ag[lo, :, cols] = total.astype(BF)

        if t in TWO:
            for i in range(4):
                own = ag.at[lo, :, cols]
                device = half_peer(i)[1] if i else dp_peer(4)[1]
                remote(own, own, ag_ss.at[t], ag_rs.at[t] if i else agp_rs.at[t], device).start()
            return

        @pl.loop(1, 8)
        def _(i):
            remote(ag.at[lo, :, cols], ag.at[lo, :, cols], ag_ss.at[t], ag_rs.at[t], dp_peer(i)[1]).start()

    def forward(t):
        cols = slice(OFFS[ORDER[t]], OFFS[ORDER[t]] + 128 * (ORDER[t] + 1))
        theirs = ag.at[dp_peer(4)[0], :, cols]
        wait_bytes(theirs, agp_rs.at[t])
        for i in range(1, 4):
            remote(theirs, theirs, ag_ss.at[t], agf_rs.at[t], half_peer(i)[1]).start()

    def ig_copy(t):
        rows = pl.ds(ORDER[t] * 128, 128)
        return pltpu.make_async_copy(ig_out.at[rows], ig_res.at[rows], out_sem.at[t])

    def ag_copy(t):
        cols = slice(OFFS[ORDER[t]], OFFS[ORDER[t]] + 128 * (ORDER[t] + 1))
        return pltpu.make_async_copy(ag.at[:, :, cols], ag_res.at[:, :, cols], out_sem.at[NI + t])

    def inner_result(t):
        cols = slice(OFFS[ORDER[t]], OFFS[ORDER[t]] + 128 * (ORDER[t] + 1))
        if t in TWO:
            wait_bytes(ag.at[pl.ds(0, 3), :, cols], ag_rs.at[t])
            wait_bytes(ag.at[pl.ds(0, 3), :, cols], agf_rs.at[t])
        else:
            wait_bytes(ag.at[pl.ds(0, 7), :, cols], ag_rs.at[t])
        ag_copy(t).start()

    @pl.when(h == 1)
    def _():
        blk[:, :8] = jnp.zeros((NI, 8, PP, CW), BF)


    outer_pass()
    outer_wait()
    for t in range(NI):
        build(ORDER[t])
    for t in range(NI - 1):
        mix(t)
        outer_part(t)
        back(t)
        back_input(t)
        if t == 2:
            exchange(0)

    own_products()
    mix(3)
    outer_part(3)
    gather(0)
    exchange(1)
    back(3)

    for a in range(4):
        src = lax.rem(y + a, 4)
        wait_bytes(sy_r.at[src], sy_rs.at[src])
    v = sy_r[0].astype(F32) + sy_r[1].astype(F32) + sy_r[2].astype(F32) + sy_r[3].astype(F32)
    ss_s[...] = v.astype(BF).reshape(8, 32, 128)

    @pl.loop(1, 8)
    def _(i):
        to, device = dp_peer(i)
        remote(ss_s.at[to], ss_r.at[lo], ss_sem.at[0], ss_sem.at[1], device).start()

    pltpu.make_async_copy(ss_s.at[lo], ss_r.at[lo], ss_sem.at[1]).start()

    gather(1)
    gather(2)
    back_input(3)
    gather(3)
    forward(0)
    forward(1)

    wait_bytes(ss_r, ss_sem.at[1])
    total = ss_r[0].astype(F32)
    for i in range(1, 8):
        total = total + ss_r[i].astype(F32)
    for hh in range(2):
        sh[hh] = jnp.concatenate([total[8 * hh:8 * hh + 8], total[16 + 8 * hh:24 + 8 * hh]], axis=0).astype(BF)
    sg[zme] = sh[h]

    @pl.loop(1, NZ)
    def _(i):
        z, device = ring_peer(i)
        remote(sh.at[z // 8], sg.at[zme], sg_sem.at[0], sg_sem.at[1], device).start()

    inner_result(0)
    inner_result(1)
    inner_result(2)

    wait_bytes(sg.at[pl.ds(0, NZ - 1)], sg_sem.at[1])
    sg_copy = pltpu.make_async_copy(sg, sg_res, out_sem.at[2 * NI])
    sg_copy.start()
    inner_result(3)

    sg_copy.wait()
    for t in range(NI):
        ig_copy(t).wait()
        ag_copy(t).wait()

    for t in range(NI):
        cols = slice(OFFS[ORDER[t]], OFFS[ORDER[t]] + 128 * (ORDER[t] + 1))
        wait_bytes(cot_s.at[t, pl.ds(0, PD - 1)], c_ss.at[t])
        wait_bytes(g_s.at[t, pl.ds(0, PD - 1)], g_ss.at[t])
        @pl.when(h == 1)
        def _():
            cross(t, 0).wait_send()

        for part in range(1, PARTS):
            cross(t, part).wait_send()
        if t in TWO:
            wait_bytes(rs_s.at[pl.ds(0, 6), :, cols], rs_ss.at[t])
            wait_bytes(ex_s.at[:, cols], ex_ss.at[t])
        else:
            wait_bytes(rs_s.at[pl.ds(0, 7), :, cols], rs_ss.at[t])
        wait_bytes(ag.at[pl.ds(0, 7), :, cols], ag_ss.at[t])

        @pl.when(y != t)
        def _():
            wait_bytes(sy_s.at[t], sy_ss.at[t])

    for a in range(7):
        wait_bytes(ot.at[0], o_ss.at[a])
    wait_bytes(x_s.at[pl.ds(0, PD - 1)], x_sem.at[0])
    wait_bytes(ss_s.at[pl.ds(0, 7)], ss_sem.at[0])
    wait_bytes(sg.at[pl.ds(0, NZ - 1)], sg_sem.at[0])


def results_kernel(
    ig_in, ag_in, sg_in, ig_out, inner_out, outer_out, ig, ag, sg, inner, spread, outer, sem
):
    scale = 1.0 / math.sqrt(8192.0)
    load_ag = pltpu.make_async_copy(ag_in, ag, sem.at[1])
    load_ag.start()
    load_sg = pltpu.make_async_copy(sg_in, sg, sem.at[2])
    load_sg.start()
    loads, wholes = [], []
    for k in range(NI):
        rows = pl.ds(k * 128, 128)
        loads.append(pltpu.make_async_copy(ig_in.at[rows], ig.at[rows], sem.at[4 + NI + k]))
        wholes.append(pltpu.make_async_copy(ig.at[rows], ig_out.at[rows], sem.at[4 + 2 * NI + k]))
        loads[-1].start()

    load_ag.wait()
    stores = []
    for k in range(NI):
        w = 128 * (k + 1)
        v = ag[:, :, OFFS[k]:OFFS[k] + w].astype(F32)
        for hh in range(2):
            start = k * 128 + hh * 64
            part = v[:, 8 * hh:8 * hh + 8, :].reshape(64, w) * scale
            keep = iota((64, w), 0) + start >= iota((64, w), 1)
            inner[start:start + 64, :w] = jnp.where(keep, part, 0.0)
            if w < B:
                inner[start:start + 64, w:] = jnp.zeros((64, B - w), F32)
        rows = pl.ds(k * 128, 128)
        stores.append(pltpu.make_async_copy(inner.at[rows], inner_out.at[rows], sem.at[3 + k]))
        stores[-1].start()
        loads[k].wait()
        wholes[k].start()

    load_sg.wait()
    parts = []
    for hs in range(2):
        parts.append(sg[hs * 8:(hs + 1) * 8].reshape(128, 128))
    c_r = iota((128, 128), 0)
    c_c = iota((128, 128), 1)
    for bh in range(4):
        v = jnp.zeros((128, 128), F32)
        for hs in range(2):
            el = c_r - 32 * bh
            col = (el >= 0) & (el < 32) & (c_c == 16 * (el // 8) + 8 * hs + lax.rem(el, 8))
            v = v + dot_nn(parts[hs], col.astype(BF))
        for g in range(2):
            base = 32 * (bh % 2) + 16 * g + 8 * (bh // 2)
            keep = iota((64, 128), 0) // 8 + base >= iota((64, 128), 1)
            spread[base * 8:base * 8 + 64] = jnp.where(keep, v[64 * g:64 * g + 64] * scale, 0.0)
    for t in range(8):
        outer[t] = spread[pl.ds(t, 64, stride=8), :][:, :64]
    last = pltpu.make_async_copy(outer, outer_out, sem.at[3 + NI])
    last.start()
    for store in stores + wholes:
        store.wait()
    last.wait()


def local(activations, cotangent, inner_weight, outer_weight):
    vmem = pl.BlockSpec(memory_space=pltpu.VMEM)
    dma = pltpu.SemaphoreType.DMA
    scratch = [
        pltpu.VMEM((B, D), BF),
        pltpu.VMEM((B, D), BF),
        pltpu.VMEM((B, B), BF),
        pltpu.VMEM((8, 64, 64), BF),
        pltpu.VMEM((NI, PD, PP, CW), BF),
        pltpu.VMEM((NI, 2 * PD, PP, CW), BF),
        pltpu.VMEM((NI, PD, PP, CW), BF),
        pltpu.VMEM((NI, PD, PP, CW), BF),
        pltpu.VMEM((PD, NI, PP, CW), BF),
        pltpu.VMEM((PD, NI, PP, CW), BF),
        pltpu.VMEM((B, B), BF),
        pltpu.VMEM((B, B), BF),
        pltpu.VMEM((128, 128), F32),
        pltpu.VMEM((2, 128, 128), BF),
        pltpu.VMEM((NI, 2, 128, 128), BF),
        pltpu.VMEM((NI, 512, 1024), BF),
        pltpu.VMEM((512, CW), F32),
        pltpu.VMEM((256, 128), F32),
        pltpu.VMEM((B, D), BF),
        pltpu.VMEM((B, D), F32),
        pltpu.VMEM((8, 16, PACK), BF),
        pltpu.VMEM((8, 16, PACK), BF),
        pltpu.VMEM((16, PACK), F32),
        pltpu.VMEM((16, PACK), BF),
        pltpu.VMEM((16, PACK), BF),
        pltpu.VMEM((8, 16, PACK), BF),
        pltpu.VMEM((NI, 256, 128), BF),
        pltpu.VMEM((NI, 256, 128), BF),
        pltpu.VMEM((8, 32, 128), BF),
        pltpu.VMEM((8, 32, 128), BF),
        pltpu.VMEM((2, 16, 128), BF),
        pltpu.VMEM((NZ, 16, 128), BF),
        dma((4,)),
        dma((NI,)), dma((NI, PARTS)),
        dma((NI, PARTS)), dma((NI, PARTS)),
        dma((2,)),
        dma((NI,)), dma((NI,)),
        dma((7,)), dma((8,)),
        dma((NI,)), dma((NI,)), dma((NI,)), dma((NI,)), dma((NI,)), dma((NI,)),
        dma((NI,)), dma((NI,)),
        dma((NI,)), dma((NI,)),
        dma((2,)), dma((2,)),
        dma((2 * NI + 1,)),
    ]
    hbm = pl.BlockSpec(memory_space=pltpu.HBM)
    sums = pl.pallas_call(
        kernel,
        out_shape=(
            jax.ShapeDtypeStruct((B, D), BF),
            jax.ShapeDtypeStruct((8, 16, PACK), BF),
            jax.ShapeDtypeStruct((NZ, 16, 128), BF),
        ),
        in_specs=[hbm] * 4,
        out_specs=(hbm, hbm, hbm),
        scratch_shapes=scratch,
        compiler_params=pltpu.CompilerParams(
            collective_id=0, has_side_effects=True, vmem_limit_bytes=62 * 1024 * 1024
        ),
        cost_estimate=pl.CostEstimate(flops=8_000_000_000, bytes_accessed=6_000_000, transcendentals=0),
        name="mixer",
    )(activations[0, 0], cotangent[0, 0], inner_weight[0], outer_weight)
    ig, inner_grad, outer_grad = pl.pallas_call(
        results_kernel,
        out_shape=(
            jax.ShapeDtypeStruct((B, D), BF),
            jax.ShapeDtypeStruct((B, B), F32),
            jax.ShapeDtypeStruct((8, 64, 64), F32),
        ),
        in_specs=[hbm] * 3,
        out_specs=(hbm, hbm, hbm),
        scratch_shapes=[
            pltpu.VMEM((B, D), BF),
            pltpu.VMEM((8, 16, PACK), BF),
            pltpu.VMEM((NZ, 16, 128), BF),
            pltpu.VMEM((B, B), F32),
            pltpu.VMEM((512, 128), F32),
            pltpu.VMEM((8, 64, 64), F32),
            dma((4 + 3 * NI,)),
        ],
        compiler_params=pltpu.CompilerParams(vmem_limit_bytes=62 * 1024 * 1024),
        cost_estimate=pl.CostEstimate(flops=50_000_000, bytes_accessed=5_000_000, transcendentals=0),
        name="results",
    )(*sums)
    return ig[None, None], inner_grad[None], outer_grad


def solution(mesh):
    placed = (
        P("dp", "seq", None, None),
        P("dp", "seq", None, None),
        P("seq", None, None),
        P("seq", None, None),
    )
    return jax.shard_map(
        local,
        mesh=mesh,
        in_specs=placed,
        out_specs=(P("dp", "seq", None, None), P("seq", None, None), P("seq", None, None)),
        check_vma=False,
    )
```

```python
import functools
import math

import jax
import jax.numpy as jnp
from jax import lax
from jax.experimental import pallas as pl
from jax.experimental.pallas import tpu as pltpu
from jax.sharding import PartitionSpec as P

MESH = pl.DeviceIdType.MESH
BF = jnp.bfloat16
F32 = jnp.float32

B = 512
D = 1024
NI = 4
CW = D // NI
PD = 32
PP = 16
NZ = 16
OFFS = (0, 128, 384, 768)
ORDER = (3, 2, 1, 0)
TWO = (0, 1)
PARTS = 4
PACK = 1280


def coords():
    lo = lax.axis_index("dp")
    s = lax.axis_index("seq")
    core = lax.rem(s, 2)
    x = lax.rem(s // 2, 4)
    h = lax.rem(s // 8, 2)
    y = s // 16
    return lo, y, h, x, core


def plane_peers():
    lo, y, h, x, core = coords()
    offs = []
    for b in range(4):
        for c in range(2):
            offs.append(lax.rem(x + b, 4) * 2 + lax.rem(core + c, 2))

    def row(a):
        py = lax.rem(y + a, 4)
        return py * 8, py * 16 + h * 8

    return row, offs, lo


def ring_peer(i):
    lo, y, h, x, core = coords()
    z = lax.rem(h * 8 + lo + i, NZ)
    return z, (lax.rem(z, 8), y * 16 + (z // 8) * 8 + x * 2 + core)


def dp_peer(i):
    lo, y, h, x, core = coords()
    t = lax.rem(lo + i, 8)
    return t, (t, y * 16 + h * 8 + x * 2 + core)


def remote(src, dst, send, recv, device):
    return pltpu.make_async_remote_copy(
        src_ref=src, dst_ref=dst, send_sem=send, recv_sem=recv, device_id=device, device_id_type=MESH
    )


def wait_bytes(ref, sem):
    pltpu.make_async_copy(ref, ref, sem).wait()


def iota(shape, dim):
    return lax.broadcasted_iota(jnp.int32, shape, dim)


def dot_nt(a, b):
    return lax.dot_general(a, b, (((1,), (1,)), ((), ())), preferred_element_type=F32)


def dot_nn(a, b):
    return lax.dot_general(a, b, (((1,), (0,)), ((), ())), preferred_element_type=F32)


def dot_tn(a, b):
    return lax.dot_general(a, b, (((0,), (0,)), ((), ())), preferred_element_type=F32)


def halves(a, b):
    first = jnp.concatenate([a[:8], b[:8]], axis=0)
    second = jnp.concatenate([a[8:], b[8:]], axis=0)
    return first.astype(BF), second.astype(BF)


def kernel(
    act_in, cot_in, inner_in, outer_in, ig_res, ag_res, sg_res,
    act, cot, inner, outer, cot_s, blk, g_s, g_r, x_s, x_r, inner_p, inner_t,
    oscr, ot, ow, wmat, g_own, s_own, ig_out, ig_acc, rs_s, rs_r, ex_m, ex_s, ex_r, ag, sy_s, sy_r, ss_s, ss_r, sh, sg,
    in_sem, c_ss, c_rs, z_ss, z_rs, x_sem, g_ss, g_rs, o_ss, o_rs, rs_ss, rs_rs, ag_ss, ag_rs, agp_rs, agf_rs, ex_ss, ex_rs,
    sy_ss, sy_rs, ss_sem, sg_sem, out_sem,
):
    lo, y, h, x, core = coords()
    me = y * 8 + x * 2 + core
    zme = h * 8 + lo
    peer_row, peer_offs, _ = plane_peers()
    mine = h * PD
    other = (1 - h) * PD

    def column_peer(a):
        py = lax.rem(y + a, 4)
        return py, (lo, py * 16 + h * 8 + x * 2 + core)

    loads = [
        pltpu.make_async_copy(a, b, in_sem.at[n])
        for n, (a, b) in enumerate(((cot_in, cot), (outer_in, outer), (inner_in, inner), (act_in, act)))
    ]
    for load in loads:
        load.start()

    barrier = pltpu.get_barrier_semaphore()

    @pl.loop(1, NZ)
    def _(i):
        pl.semaphore_signal(barrier, inc=1, device_id=ring_peer(i)[1], device_id_type=MESH)

    def plane_loop(body):
        @pl.loop(0, 4)
        def _(a):
            place, seq = peer_row(a)
            for off in peer_offs[1:]:
                body(place + off, (lo, seq + off))

        @pl.loop(1, 4)
        def _(a):
            place, seq = peer_row(a)
            body(place + peer_offs[0], (lo, seq + peer_offs[0]))

    plane_loop(lambda d, device: pl.semaphore_signal(barrier, inc=1, device_id=device, device_id_type=MESH))

    loads[0].wait()

    @pl.loop(0, 16)
    def _(q):
        big, u = q // 4, lax.rem(q, 4)
        at = pl.multiple_of(big * 128 + u * 16, 16)
        a = cot[pl.ds(at, 16), :].astype(F32)
        b = cot[pl.ds(at + 64, 16), :].astype(F32)
        first, second = halves(a, b)
        for quarter in range(4):
            cols = slice(quarter * CW, (quarter + 1) * CW)
            cot_s[big, quarter * 8 + u * 2] = first[:, cols]
            cot_s[big, quarter * 8 + u * 2 + 1] = second[:, cols]

    loads[1].wait()
    keep = iota((8, 64, 64), 1) >= iota((8, 64, 64), 2)
    factors = jnp.where(keep, outer[...].astype(F32), 0.0).astype(BF)
    lane = iota((64, 128), 1)
    el = lax.rem(lane, 32)
    for side in range(2):
        total = jnp.zeros((128, 128), F32)
        for q in range(4):
            block = 16 * (el // 8) + 8 * side + lax.rem(el, 8)
            sel = ((iota((64, 128), 0) == block) & (lane // 32 == q)).astype(BF)
            total = total + dot_nn(factors[:, 16 * q:16 * q + 16].reshape(128, 64), sel)
        for t in range(8):
            oscr[pl.ds(t, 16, stride=8), :] = total[16 * t:16 * t + 16]
        ot[side] = oscr[...].astype(BF)

    pl.semaphore_wait(barrier, PD - 1 + NZ - 1)

    def a2a_start(src, dst, send, recv):
        plane_loop(lambda d, device: remote(src(d), dst(me), send, recv, device).start())
        pltpu.make_async_copy(src(me), dst(me), recv).start()

    def cross(t, part):
        size = PD // PARTS
        rows = blk.at[ORDER[t], pl.ds(mine + part * size, size)]
        return remote(rows, rows, z_ss.at[t, part], z_rs.at[t, part], ring_peer(8)[1])

    def cross_wait(t):
        size = PD // PARTS
        @pl.when(h == 0)
        def _():
            wait_bytes(blk.at[ORDER[t], pl.ds(other, size)], z_rs.at[t, 0])

        for part in range(1, PARTS):
            wait_bytes(blk.at[ORDER[t], pl.ds(other + part * size, size)], z_rs.at[t, part])

    def own_start(t):
        k = ORDER[t]
        a2a_start(lambda d: cot_s.at[k, d], lambda d: blk.at[k, mine + d], c_ss.at[t], c_rs.at[t, y])

    def cross_when_here(t):
        size = PD // PARTS
        for a in range(PARTS):
            part = lax.rem(y + PARTS - a, PARTS)
            wait_bytes(blk.at[ORDER[t], pl.ds(mine + part * size, size)], c_rs.at[t, part])

            @pl.when(jnp.logical_or(h == 1, part > 0))
            def _():
                cross(t, part).start()

    own_start(0)
    for a in range(1, 4):
        remote(ot.at[h], ow.at[y, h], o_ss.at[a], o_rs.at[a], column_peer(a)[1]).start()
    remote(ot.at[1 - h], ow.at[y, h], o_ss.at[0], o_rs.at[0], ring_peer(8)[1]).start()
    own_copy = pltpu.make_async_copy(ot.at[h], ow.at[y, h], o_rs.at[7])
    own_copy.start()
    cross_when_here(0)
    own_start(1)
    own_start(2)
    cross_when_here(1)
    own_start(3)
    cross_when_here(2)
    cross_when_here(3)

    loads[2].wait()

    @pl.loop(0, 16)
    def _(q):
        big, u = q // 4, lax.rem(q, 4)
        at = pl.multiple_of(big * 128 + u * 16, 16)

        def rows(start):
            v = inner[pl.ds(start, 16), :].astype(F32)
            return jnp.where(iota((16, B), 0) + start >= iota((16, B), 1), v, 0.0)

        first, second = halves(rows(at), rows(at + 64))
        to = pl.multiple_of(big * 128 + u * 32, 32)
        inner_p[pl.ds(to, 16), :] = first
        inner_p[pl.ds(to + 16, 16), :] = second

    inner_t[...] = inner_p[...].T
    loads[3].wait()

    @pl.loop(0, 4)
    def _(q):
        rows = pl.ds(pl.multiple_of(q * 128, 128), 128)
        v = dot_nn(inner_p[rows, :], act[...]).astype(BF)
        for quarter in range(4):
            cols = slice(quarter * CW, (quarter + 1) * CW)
            x_s[quarter * 8:(quarter + 1) * 8, q] = v[:, cols].reshape(8, PP, CW)

    a2a_start(lambda d: x_s.at[d], lambda d: x_r.at[d], x_sem.at[0], x_sem.at[1])

    def outer_pass():
        wait_bytes(ow.at[y, 1 - h], o_rs.at[0])
        for a in range(1, 4):
            remote(ow.at[y, 1 - h], ow.at[y, 1 - h], o_ss.at[3 + a], o_rs.at[3 + a], column_peer(a)[1]).start()

    def outer_wait():
        own_copy.wait()
        for a in range(1, 4):
            src = lax.rem(y + 4 - a, 4)
            wait_bytes(ow.at[src, h], o_rs.at[a])
            wait_bytes(ow.at[src, 1 - h], o_rs.at[3 + a])

    def build(k):
        lane = iota((128, 512), 0)
        el = iota((128, 512), 1) // 16
        same = lax.rem(lane, 16) == lax.rem(iota((128, 512), 1), 16)

        @pl.loop(0, 8)
        def _(g):
            group = 2 * lax.rem(g, 4) + g // 4
            rows = pl.ds(pl.multiple_of(lax.rem(group, 2) * 64, 64), 64)
            put = (lane == 32 * (group // 2) + el).astype(BF)
            both = [dot_nn(ow[k, hh, rows, :], put).reshape(8, 8, 512) for hh in range(2)]
            w = jnp.concatenate(both, axis=1).reshape(128, 512)
            wmat[k, :, pl.ds(pl.multiple_of(g * 128, 128), 128)] = jnp.where(same, w, 0.0).astype(BF).T

    theirs = pl.ds(pl.multiple_of((1 - h) * 512, 512), 512)

    def quarters(t, half, side):
        k = ORDER[t]
        same = lax.rem(iota((128, 512), 0), 16) == lax.rem(iota((128, 512), 1), 16)
        total = jnp.zeros((128, 128), F32)
        for i in range(2):
            bh = 2 * side + i
            v = dot_nt(blk[k, pl.ds(bh * 16 + half * 8, 8)].reshape(128, CW), x_r[:, k].reshape(512, CW))
            put = (iota((512, 128), 1) == 32 * bh + iota((512, 128), 0) // 16).astype(BF)
            total = total + dot_nn(jnp.where(same, v, 0.0).astype(BF), put)
        return total

    def own_products():
        t = NI - 1
        k = ORDER[t]
        ours = pl.ds(pl.multiple_of(h * 512, 512), 512)

        @pl.loop(0, 4)
        def _(q):
            rows = pl.ds(pl.multiple_of(q * 128, 128), 128)
            g_own[rows, :] = dot_nn(wmat[k, rows, ours], blk[k, pl.ds(mine, PD)].reshape(512, CW))

        @pl.loop(0, 2)
        def _(half):
            s_own[pl.ds(pl.multiple_of(half * 128, 128), 128), :] = quarters(t, half, h)

    def mix(t):
        k = ORDER[t]
        cross_wait(t)

        @pl.loop(0, 4)
        def _(a):
            place, seq = peer_row(a)
            rows = pl.ds(pl.multiple_of(place * PP, 128), 128)
            if t == NI - 1:
                v = dot_nn(wmat[k, rows, theirs], blk[k, pl.ds(other, PD)].reshape(512, CW))
                v = (v + g_own[rows, :]).astype(BF)
            else:
                v = dot_nn(wmat[k, rows, :], blk[k].reshape(1024, CW)).astype(BF)
            g_s[k, pl.ds(place, 8)] = v.reshape(8, PP, CW)

            def give(off):
                remote(
                    g_s.at[k, place + off], g_r.at[k, me], g_ss.at[t], g_rs.at[t], (lo, seq + off)
                ).start()

            for off in peer_offs[1:]:
                give(off)

            @pl.when(a > 0)
            def _():
                give(peer_offs[0])

        pltpu.make_async_copy(g_s.at[k, me], g_r.at[k, me], g_rs.at[t]).start()

    def outer_part(t):
        k = ORDER[t]
        if t == 0:
            wait_bytes(x_r, x_sem.at[1])
        @pl.loop(0, 2)
        def _(half):
            rows = pl.ds(pl.multiple_of(half * 128, 128), 128)
            if t == NI - 1:
                total = s_own[rows, :] + quarters(t, half, 1 - h)
            else:
                total = quarters(t, half, 0) + quarters(t, half, 1)
            sy_s[k, rows, :] = total.astype(BF)

        @pl.when(y == k)
        def _():
            pltpu.make_async_copy(sy_s.at[k], sy_r.at[y], sy_rs.at[y]).start()

        @pl.when(y != k)
        def _():
            device = (lo, k * 16 + h * 8 + x * 2 + core)
            remote(sy_s.at[k], sy_r.at[y], sy_ss.at[k], sy_rs.at[y], device).start()

    def back(t):
        k = ORDER[t]
        w = 128 * (k + 1)
        wait_bytes(g_r.at[k], g_rs.at[t])
        v = jnp.zeros((128, w), F32)
        for quarter in range(4):
            cols = slice(quarter * CW, (quarter + 1) * CW)
            v = v + dot_nt(g_r[k, quarter * 8:(quarter + 1) * 8].reshape(128, CW), act[:w, cols])
        cols = slice(OFFS[k], OFFS[k] + w)
        rs_s[:, :, cols] = v.astype(BF).reshape(8, 16, w)

        if t in TWO:
            at = lax.rem(lo, 4)
            for half in (0, 4):
                for i in range(1, 4):
                    to, device = half_peer(i)
                    src = rs_s.at[lax.rem(to, 4) + half, :, cols]
                    remote(src, rs_r.at[at + half, :, cols], rs_ss.at[t], rs_rs.at[t], device).start()
                pltpu.make_async_copy(
                    rs_s.at[at + half, :, cols], rs_r.at[at + half, :, cols], rs_rs.at[t]
                ).start()
            return

        @pl.loop(1, 8)
        def _(i):
            to, device = dp_peer(i)
            remote(rs_s.at[to, :, cols], rs_r.at[lo, :, cols], rs_ss.at[t], rs_rs.at[t], device).start()

        pltpu.make_async_copy(rs_s.at[lo, :, cols], rs_r.at[lo, :, cols], rs_rs.at[t]).start()

    def exchange(t):
        cols = slice(OFFS[ORDER[t]], OFFS[ORDER[t]] + 128 * (ORDER[t] + 1))
        wait_bytes(rs_r.at[:, :, cols], rs_rs.at[t])
        sums = []
        for half in (0, 4):
            total = rs_r[half, :, cols].astype(F32)
            for i in range(1, 4):
                total = total + rs_r[half + i, :, cols].astype(F32)
            sums.append(total)
        ex_m[:, cols] = jnp.where(lo < 4, sums[0], sums[1])
        ex_s[:, cols] = jnp.where(lo < 4, sums[1], sums[0]).astype(BF)
        remote(ex_s.at[:, cols], ex_r.at[:, cols], ex_ss.at[t], ex_rs.at[t], dp_peer(4)[1]).start()

    def half_peer(i):
        to = (lo // 4) * 4 + lax.rem(lo + i, 4)
        return to, (to, y * 16 + h * 8 + x * 2 + core)

    def back_input(t):
        k = ORDER[t]
        w = 128 * (k + 1)
        for quarter in range(4):
            cols = slice(quarter * CW, (quarter + 1) * CW)
            g = g_r[k, quarter * 8:(quarter + 1) * 8].reshape(128, CW)
            v = dot_nn(inner_t[:w, k * 128:(k + 1) * 128], g)
            if t > 0:
                v = v + ig_acc[:w, cols]
            ig_out[k * 128:w, cols] = v[k * 128:].astype(BF)
            if k > 0:
                ig_acc[:k * 128, cols] = v[:k * 128]
        ig_copy(t).start()

    def gather(t):
        k = ORDER[t]
        w = 128 * (k + 1)
        cols = slice(OFFS[k], OFFS[k] + w)
        if t in TWO:
            wait_bytes(ex_r.at[:, cols], ex_rs.at[t])
            total = ex_m[:, cols] + ex_r[:, cols].astype(F32)
        else:
            wait_bytes(rs_r.at[:, :, cols], rs_rs.at[t])
            total = rs_r[0, :, cols].astype(F32)
            for i in range(1, 8):
                total = total + rs_r[i, :, cols].astype(F32)
        ag[lo, :, cols] = total.astype(BF)

        if t in TWO:
            for i in range(4):
                own = ag.at[lo, :, cols]
                device = half_peer(i)[1] if i else dp_peer(4)[1]
                remote(own, own, ag_ss.at[t], ag_rs.at[t] if i else agp_rs.at[t], device).start()
            return

        @pl.loop(1, 8)
        def _(i):
            remote(ag.at[lo, :, cols], ag.at[lo, :, cols], ag_ss.at[t], ag_rs.at[t], dp_peer(i)[1]).start()

    def forward(t):
        cols = slice(OFFS[ORDER[t]], OFFS[ORDER[t]] + 128 * (ORDER[t] + 1))
        theirs = ag.at[dp_peer(4)[0], :, cols]
        wait_bytes(theirs, agp_rs.at[t])
        for i in range(1, 4):
            remote(theirs, theirs, ag_ss.at[t], agf_rs.at[t], half_peer(i)[1]).start()

    def ig_copy(t):
        rows = pl.ds(ORDER[t] * 128, 128)
        return pltpu.make_async_copy(ig_out.at[rows], ig_res.at[rows], out_sem.at[t])

    def ag_copy(t):
        cols = slice(OFFS[ORDER[t]], OFFS[ORDER[t]] + 128 * (ORDER[t] + 1))
        return pltpu.make_async_copy(ag.at[:, :, cols], ag_res.at[:, :, cols], out_sem.at[NI + t])

    def inner_result(t):
        cols = slice(OFFS[ORDER[t]], OFFS[ORDER[t]] + 128 * (ORDER[t] + 1))
        if t in TWO:
            wait_bytes(ag.at[pl.ds(0, 3), :, cols], ag_rs.at[t])
            wait_bytes(ag.at[pl.ds(0, 3), :, cols], agf_rs.at[t])
        else:
            wait_bytes(ag.at[pl.ds(0, 7), :, cols], ag_rs.at[t])
        ag_copy(t).start()

    @pl.when(h == 1)
    def _():
        blk[:, :8] = jnp.zeros((NI, 8, PP, CW), BF)


    outer_pass()
    outer_wait()
    for t in range(NI):
        build(ORDER[t])
    for t in range(NI - 1):
        mix(t)
        outer_part(t)
        back(t)
        back_input(t)
        if t == 2:
            exchange(0)

    own_products()
    mix(3)
    outer_part(3)
    gather(0)
    exchange(1)
    back(3)

    for a in range(4):
        src = lax.rem(y + a, 4)
        wait_bytes(sy_r.at[src], sy_rs.at[src])
    v = sy_r[0].astype(F32) + sy_r[1].astype(F32) + sy_r[2].astype(F32) + sy_r[3].astype(F32)
    ss_s[...] = v.astype(BF).reshape(8, 32, 128)

    @pl.loop(1, 8)
    def _(i):
        to, device = dp_peer(i)
        remote(ss_s.at[to], ss_r.at[lo], ss_sem.at[0], ss_sem.at[1], device).start()

    pltpu.make_async_copy(ss_s.at[lo], ss_r.at[lo], ss_sem.at[1]).start()

    gather(1)
    gather(2)
    back_input(3)
    gather(3)
    forward(0)

    wait_bytes(ss_r, ss_sem.at[1])
    total = ss_r[0].astype(F32)
    for i in range(1, 8):
        total = total + ss_r[i].astype(F32)
    for hh in range(2):
        sh[hh] = jnp.concatenate([total[8 * hh:8 * hh + 8], total[16 + 8 * hh:24 + 8 * hh]], axis=0).astype(BF)
    sg[zme] = sh[h]

    @pl.loop(1, NZ)
    def _(i):
        z, device = ring_peer(i)
        remote(sh.at[z // 8], sg.at[zme], sg_sem.at[0], sg_sem.at[1], device).start()

    forward(1)
    inner_result(0)
    inner_result(1)
    inner_result(2)

    wait_bytes(sg.at[pl.ds(0, NZ - 1)], sg_sem.at[1])
    sg_copy = pltpu.make_async_copy(sg, sg_res, out_sem.at[2 * NI])
    sg_copy.start()
    inner_result(3)

    sg_copy.wait()
    for t in range(NI):
        ig_copy(t).wait()
        ag_copy(t).wait()

    for t in range(NI):
        cols = slice(OFFS[ORDER[t]], OFFS[ORDER[t]] + 128 * (ORDER[t] + 1))
        wait_bytes(cot_s.at[t, pl.ds(0, PD - 1)], c_ss.at[t])
        wait_bytes(g_s.at[t, pl.ds(0, PD - 1)], g_ss.at[t])
        @pl.when(h == 1)
        def _():
            cross(t, 0).wait_send()

        for part in range(1, PARTS):
            cross(t, part).wait_send()
        if t in TWO:
            wait_bytes(rs_s.at[pl.ds(0, 6), :, cols], rs_ss.at[t])
            wait_bytes(ex_s.at[:, cols], ex_ss.at[t])
        else:
            wait_bytes(rs_s.at[pl.ds(0, 7), :, cols], rs_ss.at[t])
        wait_bytes(ag.at[pl.ds(0, 7), :, cols], ag_ss.at[t])

        @pl.when(y != t)
        def _():
            wait_bytes(sy_s.at[t], sy_ss.at[t])

    for a in range(7):
        wait_bytes(ot.at[0], o_ss.at[a])
    wait_bytes(x_s.at[pl.ds(0, PD - 1)], x_sem.at[0])
    wait_bytes(ss_s.at[pl.ds(0, 7)], ss_sem.at[0])
    wait_bytes(sg.at[pl.ds(0, NZ - 1)], sg_sem.at[0])


def results_kernel(
    ig_in, ag_in, sg_in, ig_out, inner_out, outer_out, ig, ag, sg, inner, spread, outer, sem
):
    scale = 1.0 / math.sqrt(8192.0)
    load_ag = pltpu.make_async_copy(ag_in, ag, sem.at[1])
    load_ag.start()
    load_sg = pltpu.make_async_copy(sg_in, sg, sem.at[2])
    load_sg.start()
    loads, wholes = [], []
    for k in range(NI):
        rows = pl.ds(k * 128, 128)
        loads.append(pltpu.make_async_copy(ig_in.at[rows], ig.at[rows], sem.at[4 + NI + k]))
        wholes.append(pltpu.make_async_copy(ig.at[rows], ig_out.at[rows], sem.at[4 + 2 * NI + k]))
        loads[-1].start()

    load_ag.wait()
    stores = []
    for k in range(NI):
        w = 128 * (k + 1)
        v = ag[:, :, OFFS[k]:OFFS[k] + w].astype(F32)
        for hh in range(2):
            start = k * 128 + hh * 64
            part = v[:, 8 * hh:8 * hh + 8, :].reshape(64, w) * scale
            keep = iota((64, w), 0) + start >= iota((64, w), 1)
            inner[start:start + 64, :w] = jnp.where(keep, part, 0.0)
            if w < B:
                inner[start:start + 64, w:] = jnp.zeros((64, B - w), F32)
        rows = pl.ds(k * 128, 128)
        stores.append(pltpu.make_async_copy(inner.at[rows], inner_out.at[rows], sem.at[3 + k]))
        stores[-1].start()
        loads[k].wait()
        wholes[k].start()

    load_sg.wait()
    parts = []
    for hs in range(2):
        parts.append(sg[hs * 8:(hs + 1) * 8].reshape(128, 128))
    c_r = iota((128, 128), 0)
    c_c = iota((128, 128), 1)
    for bh in range(4):
        v = jnp.zeros((128, 128), F32)
        for hs in range(2):
            el = c_r - 32 * bh
            col = (el >= 0) & (el < 32) & (c_c == 16 * (el // 8) + 8 * hs + lax.rem(el, 8))
            v = v + dot_nn(parts[hs], col.astype(BF))
        for g in range(2):
            base = 32 * (bh % 2) + 16 * g + 8 * (bh // 2)
            keep = iota((64, 128), 0) // 8 + base >= iota((64, 128), 1)
            spread[base * 8:base * 8 + 64] = jnp.where(keep, v[64 * g:64 * g + 64] * scale, 0.0)
    for t in range(8):
        outer[t] = spread[pl.ds(t, 64, stride=8), :][:, :64]
    last = pltpu.make_async_copy(outer, outer_out, sem.at[3 + NI])
    last.start()
    for store in stores + wholes:
        store.wait()
    last.wait()


def local(activations, cotangent, inner_weight, outer_weight):
    vmem = pl.BlockSpec(memory_space=pltpu.VMEM)
    dma = pltpu.SemaphoreType.DMA
    scratch = [
        pltpu.VMEM((B, D), BF),
        pltpu.VMEM((B, D), BF),
        pltpu.VMEM((B, B), BF),
        pltpu.VMEM((8, 64, 64), BF),
        pltpu.VMEM((NI, PD, PP, CW), BF),
        pltpu.VMEM((NI, 2 * PD, PP, CW), BF),
        pltpu.VMEM((NI, PD, PP, CW), BF),
        pltpu.VMEM((NI, PD, PP, CW), BF),
        pltpu.VMEM((PD, NI, PP, CW), BF),
        pltpu.VMEM((PD, NI, PP, CW), BF),
        pltpu.VMEM((B, B), BF),
        pltpu.VMEM((B, B), BF),
        pltpu.VMEM((128, 128), F32),
        pltpu.VMEM((2, 128, 128), BF),
        pltpu.VMEM((NI, 2, 128, 128), BF),
        pltpu.VMEM((NI, 512, 1024), BF),
        pltpu.VMEM((512, CW), F32),
        pltpu.VMEM((256, 128), F32),
        pltpu.VMEM((B, D), BF),
        pltpu.VMEM((B, D), F32),
        pltpu.VMEM((8, 16, PACK), BF),
        pltpu.VMEM((8, 16, PACK), BF),
        pltpu.VMEM((16, PACK), F32),
        pltpu.VMEM((16, PACK), BF),
        pltpu.VMEM((16, PACK), BF),
        pltpu.VMEM((8, 16, PACK), BF),
        pltpu.VMEM((NI, 256, 128), BF),
        pltpu.VMEM((NI, 256, 128), BF),
        pltpu.VMEM((8, 32, 128), BF),
        pltpu.VMEM((8, 32, 128), BF),
        pltpu.VMEM((2, 16, 128), BF),
        pltpu.VMEM((NZ, 16, 128), BF),
        dma((4,)),
        dma((NI,)), dma((NI, PARTS)),
        dma((NI, PARTS)), dma((NI, PARTS)),
        dma((2,)),
        dma((NI,)), dma((NI,)),
        dma((7,)), dma((8,)),
        dma((NI,)), dma((NI,)), dma((NI,)), dma((NI,)), dma((NI,)), dma((NI,)),
        dma((NI,)), dma((NI,)),
        dma((NI,)), dma((NI,)),
        dma((2,)), dma((2,)),
        dma((2 * NI + 1,)),
    ]
    hbm = pl.BlockSpec(memory_space=pltpu.HBM)
    sums = pl.pallas_call(
        kernel,
        out_shape=(
            jax.ShapeDtypeStruct((B, D), BF),
            jax.ShapeDtypeStruct((8, 16, PACK), BF),
            jax.ShapeDtypeStruct((NZ, 16, 128), BF),
        ),
        in_specs=[hbm] * 4,
        out_specs=(hbm, hbm, hbm),
        scratch_shapes=scratch,
        compiler_params=pltpu.CompilerParams(
            collective_id=0, has_side_effects=True, vmem_limit_bytes=62 * 1024 * 1024
        ),
        cost_estimate=pl.CostEstimate(flops=8_000_000_000, bytes_accessed=6_000_000, transcendentals=0),
        name="mixer",
    )(activations[0, 0], cotangent[0, 0], inner_weight[0], outer_weight)
    ig, inner_grad, outer_grad = pl.pallas_call(
        results_kernel,
        out_shape=(
            jax.ShapeDtypeStruct((B, D), BF),
            jax.ShapeDtypeStruct((B, B), F32),
            jax.ShapeDtypeStruct((8, 64, 64), F32),
        ),
        in_specs=[hbm] * 3,
        out_specs=(hbm, hbm, hbm),
        scratch_shapes=[
            pltpu.VMEM((B, D), BF),
            pltpu.VMEM((8, 16, PACK), BF),
            pltpu.VMEM((NZ, 16, 128), BF),
            pltpu.VMEM((B, B), F32),
            pltpu.VMEM((512, 128), F32),
            pltpu.VMEM((8, 64, 64), F32),
            dma((4 + 3 * NI,)),
        ],
        compiler_params=pltpu.CompilerParams(vmem_limit_bytes=62 * 1024 * 1024),
        cost_estimate=pl.CostEstimate(flops=50_000_000, bytes_accessed=5_000_000, transcendentals=0),
        name="results",
    )(*sums)
    return ig[None, None], inner_grad[None], outer_grad


def solution(mesh):
    placed = (
        P("dp", "seq", None, None),
        P("dp", "seq", None, None),
        P("seq", None, None),
        P("seq", None, None),
    )
    return jax.shard_map(
        local,
        mesh=mesh,
        in_specs=placed,
        out_specs=(P("dp", "seq", None, None), P("seq", None, None), P("seq", None, None)),
        check_vma=False,
    )
```
